32 devices in a mesh: groups: 2 (over y), row: 8 (over z, x), col: 2 (over core).
Axes of the slice: x: 2, y: 2, z: 4, core: 2. Of those that a mesh axis runs over, the one named last changes fastest.
Arguments:
- inductance: float32 [2048, 16384], P(('groups', 'col'), 'row'), parts along dimension 0, may hold values from -0.0625 to 0.0625
- current_rates: float32 [16384, 4096], P('row', ('groups', 'col')), parts along dimension 1, may hold values from -6 to 6
Outputs:
- induced_voltage: float32 [1024, 4096], P('row', ('groups', 'col')), parts along dimension 1
The draws below stay inside these ranges and needn't reach their ends.
There are 2 independent parts, one for each index of `groups`. The reference program is written for one: setup_inputs(seed, part) draws one part's arguments, and reference() takes and returns one part's arrays. A program takes and returns all parts, laid end to end along the dimension named above; each array names one. Nothing has to cross between parts.
All inputs are finite; a program needn't handle non-finite values.
Results may differ from the reference program's by a relative error of at most 0.000071.
Values sent between devices are 32-bit elements; how exact they have to be, the bound alone decides.
No kernel may reach another device: no remote copies, remote signals or barrier semaphores. Data moves between devices by JAX's collectives and lax.ppermute only.
A program may use at most 64 MiB of HBM per device.

```python
import jax
import jax.numpy as jnp
from jax import lax

M = 16384
P_SIZE = 2048
R = 1024


def with_spikes(drawn, rng, source, target, blocks, factor):
    owner, partner = [(jnp.arange(drawn.shape[position]) // (drawn.shape[position] // blocks)).reshape([-1 if axis == position else 1 for axis in range(drawn.ndim)]) for position in (source, target)]
    chosen = jax.random.permutation(rng, blocks)[partner]
    strong = (owner == chosen) | (owner == (partner + blocks // 2) % blocks)
    return jnp.where(strong, factor * drawn, drawn)


def block_scale(stream_key, dims, split, smallest, largest):
    def one(axis_at, parts):
        steps = jax.random.uniform(jax.random.fold_in(jax.random.fold_in(stream_key, 6), axis_at), (parts,), jnp.float32, smallest / len(split), largest / len(split))
        return jnp.repeat(jnp.exp(steps), dims[axis_at] // parts).reshape((-1,) + (1,) * (len(dims) - axis_at - 1))

    factor_of = one(*split[0])
    for cut in split[1:]:
        factor_of = factor_of * one(*cut)
    return factor_of


def gaussian(own_key, extent, spread, bound, cuts=(), kind=jnp.bfloat16):
    entries = spread * jax.random.normal(own_key, extent, jnp.float32)
    if cuts:
        entries = entries * block_scale(own_key, extent, cuts, -0.22, 0.18)
    return jnp.clip(entries, -bound, bound).astype(kind)


def bell_draw_with(stream_key, dims, deviation, bound, shards, heavy, kind=jnp.bfloat16):
    array = deviation * jax.random.normal(stream_key, dims, jnp.float32)
    if shards:
        array = array * block_scale(stream_key, dims, shards, -0.22, 0.18)
    return jnp.clip(with_spikes(array, jax.random.fold_in(stream_key, 3), *heavy), -bound, bound).astype(kind)


def setup_inputs(seed: int = 0, part: int = 0) -> dict:
    arg_keys = jax.random.split(jax.random.key(seed), 3)
    part_splits = jax.random.split(jax.random.fold_in(arg_keys[2], part), 3)
    return {
        "inductance": bell_draw_with(part_splits[0], (R, M), M ** -0.5, 0.0625, ((0, 2), (1, 8)), (1, 0, 8, 2.0), jnp.float32),
        "current_rates": gaussian(part_splits[1], (M, P_SIZE), 1.0, 6.0, ((0, 8), (1, 2)), jnp.float32),
    }


def reference(inductance, current_rates):
    coupling = jnp.dot(inductance, current_rates, precision=lax.Precision.HIGHEST, preferred_element_type=jnp.float32)
    return coupling
```

```python
import jax
import jax.numpy as jnp
import numpy as np
from jax import lax
from jax.sharding import PartitionSpec as P


def product(left, right):
    return jnp.dot(left, right, precision=lax.Precision.HIGH, preferred_element_type=jnp.float32)


def ring_order(mesh):
    count = mesh.shape["row"]
    axes = list(mesh.axis_names)
    line = np.moveaxis(mesh.devices, axes.index("row"), 0).reshape(count, -1)[:, 0]
    spots = [tuple(device.coords) for device in line]
    moving = [axis for axis in range(3) if len({spot[axis] for spot in spots}) > 1]
    plain = list(range(count))
    if len(moving) != 2:
        return plain
    for outer, inner in (moving, moving[::-1]):
        across = sorted({spot[outer] for spot in spots})
        along = sorted({spot[inner] for spot in spots})
        if len(across) % 2 or len(across) * len(along) != count:
            continue
        at = {(spot[outer], spot[inner]): index for index, spot in enumerate(spots)}
        walk = [at[across[0], along[0]]]
        for turn, a in enumerate(across):
            rest = along[1:]
            walk += [at[a, b] for b in (rest if turn % 2 == 0 else rest[::-1])]
        walk += [at[a, along[0]] for a in across[:0:-1]]
        return walk
    return plain


def solution(mesh):
    rows = mesh.shape["row"]
    cols = mesh.shape["col"]
    order = ring_order(mesh)
    place = np.zeros(rows, np.int32)
    place[order] = np.arange(rows)
    swap = [(core, cols - 1 - core) for core in range(cols)]
    ahead = [(order[i], order[(i + 1) % rows]) for i in range(rows)]
    behind = [(order[i], order[(i - 1) % rows]) for i in range(rows)]

    def shards(inductance, current_rates):
        held = inductance.shape[0]
        size = held * cols // rows
        half = size // 2
        mine = lax.axis_index("col")
        spot = jnp.asarray(place)[lax.axis_index("row")]
        walk = jnp.asarray(np.array(order, np.int32))
        other = lax.ppermute(inductance, "col", swap)
        partial = jnp.concatenate([product(inductance, current_rates), product(other, current_rates)])

        def block(step, side):
            target = walk[(spot + step + rows) % rows]
            start = (target * size + mine * held) % (cols * held) + side * half
            return lax.dynamic_slice_in_dim(partial, start, half)

        up, down = block(-1, 0), block(1, 1)
        for step in range(1, rows):
            up = lax.ppermute(up, "row", ahead) + block(-1 - step, 0)
            down = lax.ppermute(down, "row", behind) + block(1 + step, 1)
        return jnp.concatenate([up, down])

    placed = (P(("groups", "col"), "row"), P("row", ("groups", "col")))
    return jax.shard_map(
        shards, mesh=mesh, in_specs=placed, out_specs=P("row", ("groups", "col")), check_vma=False
    )
```

```python
import functools

import jax
import jax.numpy as jnp
import numpy as np
from jax import lax
from jax.experimental import pallas as pl
from jax.experimental.pallas import tpu as pltpu
from jax.sharding import PartitionSpec as P

CALLS = 8
LANES = 256


def ring_order(mesh):
    count = mesh.shape["row"]
    axes = list(mesh.axis_names)
    line = np.moveaxis(mesh.devices, axes.index("row"), 0).reshape(count, -1)[:, 0]
    spots = [tuple(device.coords) for device in line]
    moving = [axis for axis in range(3) if len({spot[axis] for spot in spots}) > 1]
    plain = list(range(count))
    if len(moving) != 2:
        return plain
    for outer, inner in (moving, moving[::-1]):
        across = sorted({spot[outer] for spot in spots})
        along = sorted({spot[inner] for spot in spots})
        if len(across) % 2 or len(across) * len(along) != count:
            continue
        at = {(spot[outer], spot[inner]): index for index, spot in enumerate(spots)}
        walk = [at[across[0], along[0]]]
        for turn, a in enumerate(across):
            rest = along[1:]
            walk += [at[a, b] for b in (rest if turn % 2 == 0 else rest[::-1])]
        walk += [at[a, along[0]] for a in across[:0:-1]]
        return walk
    return plain


def looked_up(table):
    row, col = lax.axis_index("row"), lax.axis_index("col")
    found = jnp.int32(0)
    for r in range(table.shape[0]):
        for c in range(table.shape[1]):
            found = jnp.where((row == r) & (col == c), jnp.int32(table[r, c]), found)
    return found


def pick_kernel(starts, size, a_ref, out_ref, sems):
    copies = []
    for index in range(starts.shape[-1]):
        start = pl.multiple_of(looked_up(starts[..., index]), size)
        copies.append(
            pltpu.make_async_copy(
                a_ref.at[pl.ds(start, size)], out_ref.at[pl.ds(index * size, size)], sems.at[index]
            )
        )
    for copy in copies:
        copy.start()
    for copy in copies:
        copy.wait()


def pick(inductance, starts, size):
    count = starts.shape[-1]
    width = inductance.shape[1]
    return pl.pallas_call(
        functools.partial(pick_kernel, starts, size),
        out_shape=jax.ShapeDtypeStruct((count * size, width), jnp.float32),
        in_specs=[pl.BlockSpec(memory_space=pl.ANY)],
        out_specs=pl.BlockSpec(memory_space=pl.ANY),
        scratch_shapes=[pltpu.SemaphoreType.DMA((count,))],
        cost_estimate=pl.CostEstimate(flops=0, bytes_accessed=8 * count * size * width, transcendentals=0),
        name="pick",
    )(inductance)


def halves(value):
    high = value.astype(jnp.bfloat16)
    return high, (value - high.astype(jnp.float32)).astype(jnp.bfloat16)


def split_kernel(value_ref, high_ref, low_ref):
    high_ref[...], low_ref[...] = halves(value_ref[...])


def split(current_rates, part, parts):
    depth, width = current_rates.shape
    width //= parts
    tile = 256
    out = jax.ShapeDtypeStruct((depth, width), jnp.bfloat16)
    return pl.pallas_call(
        split_kernel,
        grid=(depth // tile,),
        out_shape=(out, out),
        in_specs=[pl.BlockSpec((tile, width), lambda k: (k, part))],
        out_specs=[pl.BlockSpec((tile, width), lambda k: (k, 0))] * 2,
        cost_estimate=pl.CostEstimate(flops=4 * depth * width, bytes_accessed=8 * depth * width, transcendentals=0),
        name="split",
    )(current_rates)


def product_kernel(starts, size, bounds, *refs):
    count = len(bounds)
    sources, (high_ref, low_ref, out_ref, raw, stack, sems) = refs[:count], refs[count:]
    depth = raw.shape[0]

    @pl.when(pl.program_id(0) == 0)
    def _():
        for index in range(starts.shape[-1]):
            start = looked_up(starts[..., index])
            first = 0
            for source, last in zip(sources, bounds):

                @pl.when((start >= first) & (start < last))
                def _(source=source, first=first, start=start, index=index):
                    pltpu.make_async_copy(
                        source.at[pl.ds(pl.multiple_of(start - first, size), size)],
                        raw.at[pl.ds(index * size, size)],
                        sems.at[index],
                    ).start()

                first = last
        for index in range(starts.shape[-1]):
            pltpu.make_async_copy(
                sources[0].at[pl.ds(0, size)], raw.at[pl.ds(index * size, size)], sems.at[index]
            ).wait()
        stack[:depth], stack[depth:] = halves(raw[...])

    both = jnp.dot(stack[...], high_ref[...], preferred_element_type=jnp.float32)
    rest = jnp.dot(stack[:depth], low_ref[...], preferred_element_type=jnp.float32)
    out_ref[...] = both[:depth] + (both[depth:] + rest)


def product(sources, starts, size, high, low):
    depth = starts.shape[-1] * size
    inner, width = high.shape
    tile = min(LANES, width)
    return pl.pallas_call(
        functools.partial(product_kernel, starts, size, list(np.cumsum([s.shape[0] for s in sources]))),
        grid=(width // tile,),
        out_shape=jax.ShapeDtypeStruct((depth, width), jnp.float32),
        in_specs=[pl.BlockSpec(memory_space=pl.ANY)] * len(sources)
        + [pl.BlockSpec((inner, tile), lambda j: (0, j))] * 2,
        out_specs=pl.BlockSpec((depth, tile), lambda j: (0, j)),
        scratch_shapes=[
            pltpu.VMEM((depth, inner), jnp.float32),
            pltpu.VMEM((2 * depth, inner), jnp.bfloat16),
            pltpu.SemaphoreType.DMA((starts.shape[-1],)),
        ],
        compiler_params=pltpu.CompilerParams(vmem_limit_bytes=16 * 2**20),
        cost_estimate=pl.CostEstimate(
            flops=6 * depth * inner * width,
            bytes_accessed=4 * depth * inner + 4 * inner * width + 4 * depth * width,
            transcendentals=0,
        ),
        name="product",
    )(*sources, high, low)


def plan(order, rows, cols, size):
    place = np.zeros(rows, np.int64)
    place[order] = np.arange(rows)
    each = rows // cols
    needs = np.zeros((rows, cols, rows), np.int64)
    for row in range(rows):
        for core in range(cols):
            way = -1 if core == 0 else 1
            needs[row, core] = [order[(place[row] + way * (k + 1)) % rows] for k in range(rows)]
    taken = np.zeros((rows, cols, rows), np.int64)
    given = np.zeros((rows, cols, each), np.int64)
    for row in range(rows):
        for core in range(cols):
            arrived = 0
            for k, block in enumerate(needs[row, core]):
                if block // each == core:
                    taken[row, core, k] = (block - core * each) * size
                else:
                    taken[row, core, k] = (each + arrived) * size
                    arrived += 1
            wanted = [block for block in needs[row, 1 - core] if block // each == core]
            given[row, core] = [(block - core * each) * size for block in wanted]
    return taken, given


def solution(mesh):
    rows, cols = mesh.shape["row"], mesh.shape["col"]
    order = ring_order(mesh)
    group = max(rows // CALLS, 1)
    swap = [(core, cols - 1 - core) for core in range(cols)]
    around = [
        (order[i] * cols + core, order[(i + (1 if core == 0 else -1)) % rows] * cols + core)
        for i in range(rows)
        for core in range(cols)
    ]

    def shards(inductance, current_rates):
        size = inductance.shape[0] * cols // rows
        taken, given = plan(order, rows, cols, size)
        soon = lax.ppermute(pick(inductance, given[..., :group], size), "col", swap)
        late = lax.ppermute(pick(inductance, given[..., group:], size), "col", swap)
        rates = [split(current_rates, part, 2) for part in range(2)]
        first = [product([inductance, soon], taken[..., :group], size, *pair) for pair in rates]
        sums = [part[:size] for part in first]
        for step in range(1, rows):
            passed = [lax.ppermute(part, ("row", "col"), around) for part in sums]
            if step % group == 0:
                starts = taken[..., step : step + group]
                first = [product([inductance, soon, late], starts, size, *pair) for pair in rates]
            at = step % group * size
            sums = [got + part[at : at + size] for got, part in zip(passed, first)]
        return jnp.concatenate(sums, axis=1)

    placed = (P(("groups", "col"), "row"), P("row", ("groups", "col")))
    return jax.shard_map(
        shards, mesh=mesh, in_specs=placed, out_specs=P("row", ("groups", "col")), check_vma=False
    )
```

```python
import functools

import jax
import jax.numpy as jnp
import numpy as np
from jax import lax
from jax.experimental import pallas as pl
from jax.experimental.pallas import tpu as pltpu
from jax.sharding import PartitionSpec as P

CALLS = 8
LANES = 256


def ring_order(mesh):
    count = mesh.shape["row"]
    axes = list(mesh.axis_names)
    line = np.moveaxis(mesh.devices, axes.index("row"), 0).reshape(count, -1)[:, 0]
    spots = [tuple(device.coords) for device in line]
    moving = [axis for axis in range(3) if len({spot[axis] for spot in spots}) > 1]
    plain = list(range(count))
    if len(moving) != 2:
        return plain
    for outer, inner in (moving, moving[::-1]):
        across = sorted({spot[outer] for spot in spots})
        along = sorted({spot[inner] for spot in spots})
        if len(across) % 2 or len(across) * len(along) != count:
            continue
        at = {(spot[outer], spot[inner]): index for index, spot in enumerate(spots)}
        walk = [at[across[0], along[0]]]
        for turn, a in enumerate(across):
            rest = along[1:]
            walk += [at[a, b] for b in (rest if turn % 2 == 0 else rest[::-1])]
        walk += [at[a, along[0]] for a in across[:0:-1]]
        return walk
    return plain


def looked_up(table):
    row, col = lax.axis_index("row"), lax.axis_index("col")
    found = jnp.int32(0)
    for r in range(table.shape[0]):
        for c in range(table.shape[1]):
            found = jnp.where((row == r) & (col == c), jnp.int32(table[r, c]), found)
    return found


def pick_kernel(starts, size, a_ref, *refs):
    out_ref, sems = refs[-2:]
    copies = []
    for index in range(starts.shape[-1]):
        start = pl.multiple_of(looked_up(starts[..., index]), size)
        copies.append(
            pltpu.make_async_copy(
                a_ref.at[pl.ds(start, size)], out_ref.at[pl.ds(index * size, size)], sems.at[index]
            )
        )
    for copy in copies:
        copy.start()
    for copy in copies:
        copy.wait()


def pick(inductance, starts, size, *after):
    count = starts.shape[-1]
    width = inductance.shape[1]
    return pl.pallas_call(
        functools.partial(pick_kernel, starts, size),
        out_shape=jax.ShapeDtypeStruct((count * size, width), jnp.float32),
        in_specs=[pl.BlockSpec(memory_space=pl.ANY)] * (1 + len(after)),
        out_specs=pl.BlockSpec(memory_space=pltpu.VMEM),
        scratch_shapes=[pltpu.SemaphoreType.DMA((count,))],
        compiler_params=pltpu.CompilerParams(vmem_limit_bytes=8 * 2**20),
        cost_estimate=pl.CostEstimate(flops=0, bytes_accessed=8 * count * size * width, transcendentals=0),
        name="pick",
    )(inductance, *after)


def halves(value):
    high = value.astype(jnp.bfloat16)
    return high, (value - high.astype(jnp.float32)).astype(jnp.bfloat16)


def split_kernel(value_ref, high_ref, low_ref):
    high_ref[...], low_ref[...] = halves(value_ref[...])


def split(current_rates, part, parts):
    depth, width = current_rates.shape
    width //= parts
    tile = min(512, depth)
    out = jax.ShapeDtypeStruct((depth, width), jnp.bfloat16)
    return pl.pallas_call(
        split_kernel,
        grid=(depth // tile,),
        out_shape=(out, out),
        in_specs=[pl.BlockSpec((tile, width), lambda k: (k, part))],
        out_specs=[pl.BlockSpec((tile, width), lambda k: (k, 0))] * 2,
        compiler_params=pltpu.CompilerParams(vmem_limit_bytes=8 * 2**20),
        cost_estimate=pl.CostEstimate(flops=4 * depth * width, bytes_accessed=8 * depth * width, transcendentals=0),
        name="split",
    )(current_rates)


def product_kernel(starts, size, bounds, parts, *refs):
    count = len(bounds)
    sources, pairs, outs = refs[:count], refs[count : count + 2 * parts], refs[count + 2 * parts : -3]
    raw, stack, sems = refs[-3:]
    depth = raw.shape[0]
    for index in range(starts.shape[-1]):
        start = looked_up(starts[..., index])
        first = 0
        for source, last in zip(sources, bounds):

            @pl.when((start >= first) & (start < last))
            def _(source=source, first=first, start=start, index=index):
                pltpu.make_async_copy(
                    source.at[pl.ds(pl.multiple_of(start - first, size), size)],
                    raw.at[pl.ds(index * size, size)],
                    sems.at[index],
                ).start()

            first = last
    for index in range(starts.shape[-1]):
        pltpu.make_async_copy(
            sources[0].at[pl.ds(0, size)], raw.at[pl.ds(index * size, size)], sems.at[index]
        ).wait()
    stack[:depth], stack[depth:] = halves(raw[...])
    for part in range(parts):
        high_ref, low_ref, out_ref = pairs[2 * part], pairs[2 * part + 1], outs[part]
        width = out_ref.shape[1]
        tile = min(LANES, width)
        for at in range(0, width, tile):
            both = jnp.dot(stack[...], high_ref[:, at : at + tile], preferred_element_type=jnp.float32)
            rest = jnp.dot(stack[:depth], low_ref[:, at : at + tile], preferred_element_type=jnp.float32)
            out_ref[:, at : at + tile] = both[:depth] + (both[depth:] + rest)


def product(sources, starts, size, pairs):
    depth = starts.shape[-1] * size
    inner, width = pairs[0].shape
    parts = len(pairs) // 2
    return pl.pallas_call(
        functools.partial(product_kernel, starts, size, list(np.cumsum([s.shape[0] for s in sources])), parts),
        out_shape=[jax.ShapeDtypeStruct((depth, width), jnp.float32)] * parts,
        in_specs=[pl.BlockSpec(memory_space=pl.ANY)] * len(sources)
        + [pl.BlockSpec(memory_space=pltpu.VMEM)] * len(pairs),
        out_specs=[pl.BlockSpec(memory_space=pltpu.VMEM)] * parts,
        scratch_shapes=[
            pltpu.VMEM((depth, inner), jnp.float32),
            pltpu.VMEM((2 * depth, inner), jnp.bfloat16),
            pltpu.SemaphoreType.DMA((starts.shape[-1],)),
        ],
        compiler_params=pltpu.CompilerParams(vmem_limit_bytes=16 * 2**20),
        cost_estimate=pl.CostEstimate(
            flops=6 * depth * inner * width * parts,
            bytes_accessed=4 * depth * inner + 4 * inner * width * parts + 4 * depth * width * parts,
            transcendentals=0,
        ),
        name="product",
    )(*sources, *pairs)


def plan(order, rows, cols, size):
    place = np.zeros(rows, np.int64)
    place[order] = np.arange(rows)
    each = rows // cols
    needs = np.zeros((rows, cols, rows), np.int64)
    for row in range(rows):
        for core in range(cols):
            way = -1 if core == 0 else 1
            needs[row, core] = [order[(place[row] + way * (k + 1)) % rows] for k in range(rows)]
    taken = np.zeros((rows, cols, rows), np.int64)
    given = np.zeros((rows, cols, each), np.int64)
    for row in range(rows):
        for core in range(cols):
            arrived = 0
            for k, block in enumerate(needs[row, core]):
                if block // each == core:
                    taken[row, core, k] = (block - core * each) * size
                else:
                    taken[row, core, k] = (each + arrived) * size
                    arrived += 1
            wanted = [block for block in needs[row, 1 - core] if block // each == core]
            given[row, core] = [(block - core * each) * size for block in wanted]
    return taken, given


def solution(mesh):
    rows, cols = mesh.shape["row"], mesh.shape["col"]
    order = ring_order(mesh)
    group = max(rows // CALLS, 1)
    swap = [(core, cols - 1 - core) for core in range(cols)]
    around = [
        (order[i] * cols + core, order[(i + (1 if core == 0 else -1)) % rows] * cols + core)
        for i in range(rows)
        for core in range(cols)
    ]

    def shards(inductance, current_rates):
        size = inductance.shape[0] * cols // rows
        taken, given = plan(order, rows, cols, size)
        picked = pick(inductance, given[..., :group], size)
        soon = lax.ppermute(picked, "col", swap)
        late = lax.ppermute(pick(inductance, given[..., group:], size, picked), "col", swap)
        rates = [split(current_rates, part, 2) for part in range(2)]
        terms = [product([inductance, soon], taken[..., :group], size, pair)[0] for pair in rates]
        sums = [term[:size] for term in terms]
        for step in range(1, rows):
            passed = [lax.ppermute(part, ("row", "col"), around) for part in sums]
            if step % group == 0:
                starts = taken[..., step : step + group]
                terms = product([inductance, soon, late], starts, size, rates[0] + rates[1])
            at = step % group * size
            sums = [got + term[at : at + size] for got, term in zip(passed, terms)]
        return jnp.concatenate(sums, axis=1)

    placed = (P(("groups", "col"), "row"), P("row", ("groups", "col")))
    return jax.shard_map(
        shards, mesh=mesh, in_specs=placed, out_specs=P("row", ("groups", "col")), check_vma=False
    )
```

```python
import functools

import jax
import jax.numpy as jnp
import numpy as np
from jax import lax
from jax.experimental import pallas as pl
from jax.experimental.pallas import tpu as pltpu
from jax.sharding import PartitionSpec as P

CALLS = 8
LANES = 256


def ring_order(mesh):
    count = mesh.shape["row"]
    axes = list(mesh.axis_names)
    line = np.moveaxis(mesh.devices, axes.index("row"), 0).reshape(count, -1)[:, 0]
    spots = [tuple(device.coords) for device in line]
    moving = [axis for axis in range(3) if len({spot[axis] for spot in spots}) > 1]
    plain = list(range(count))
    if len(moving) != 2:
        return plain
    for outer, inner in (moving, moving[::-1]):
        across = sorted({spot[outer] for spot in spots})
        along = sorted({spot[inner] for spot in spots})
        if len(across) % 2 or len(across) * len(along) != count:
            continue
        at = {(spot[outer], spot[inner]): index for index, spot in enumerate(spots)}
        walk = [at[across[0], along[0]]]
        for turn, a in enumerate(across):
            rest = along[1:]
            walk += [at[a, b] for b in (rest if turn % 2 == 0 else rest[::-1])]
        walk += [at[a, along[0]] for a in across[:0:-1]]
        return walk
    return plain


def looked_up(table):
    row, col = lax.axis_index("row"), lax.axis_index("col")
    found = jnp.int32(0)
    for r in range(table.shape[0]):
        for c in range(table.shape[1]):
            found = jnp.where((row == r) & (col == c), jnp.int32(table[r, c]), found)
    return found


def pick_kernel(starts, size, a_ref, *refs):
    out_ref, sems = refs[-2:]
    copies = []
    for index in range(starts.shape[-1]):
        start = pl.multiple_of(looked_up(starts[..., index]), size)
        copies.append(
            pltpu.make_async_copy(
                a_ref.at[pl.ds(start, size)], out_ref.at[pl.ds(index * size, size)], sems.at[index]
            )
        )
    for copy in copies:
        copy.start()
    for copy in copies:
        copy.wait()


def pick(inductance, starts, size, *after):
    count = starts.shape[-1]
    width = inductance.shape[1]
    return pl.pallas_call(
        functools.partial(pick_kernel, starts, size),
        out_shape=jax.ShapeDtypeStruct((count * size, width), jnp.float32),
        in_specs=[pl.BlockSpec(memory_space=pl.ANY)] * (1 + len(after)),
        out_specs=pl.BlockSpec(memory_space=pltpu.VMEM),
        scratch_shapes=[pltpu.SemaphoreType.DMA((count,))],
        compiler_params=pltpu.CompilerParams(vmem_limit_bytes=8 * 2**20),
        cost_estimate=pl.CostEstimate(flops=0, bytes_accessed=8 * count * size * width, transcendentals=0),
        name="pick",
    )(inductance, *after)


def halves(value):
    high = value.astype(jnp.bfloat16)
    return high, (value - high.astype(jnp.float32)).astype(jnp.bfloat16)


def split_kernel(value_ref, high_ref, low_ref):
    high_ref[...], low_ref[...] = halves(value_ref[...])


def split(current_rates):
    depth, width = current_rates.shape
    tile = min(512, depth)
    out = jax.ShapeDtypeStruct((depth, width), jnp.bfloat16)
    return pl.pallas_call(
        split_kernel,
        grid=(depth // tile,),
        out_shape=(out, out),
        in_specs=[pl.BlockSpec((tile, width), lambda k: (k, 0))],
        out_specs=[pl.BlockSpec((tile, width), lambda k: (k, 0))] * 2,
        compiler_params=pltpu.CompilerParams(vmem_limit_bytes=12 * 2**20),
        cost_estimate=pl.CostEstimate(flops=4 * depth * width, bytes_accessed=8 * depth * width, transcendentals=0),
        name="split",
    )(current_rates)


def product_kernel(starts, size, bounds, cuts, *refs):
    count = len(bounds)
    sources, (high_ref, low_ref), outs = refs[:count], refs[count : count + 2], refs[count + 2 : -3]
    raw, stack, sems = refs[-3:]
    depth = raw.shape[0]
    for index in range(starts.shape[-1]):
        start = looked_up(starts[..., index])
        first = 0
        for source, last in zip(sources, bounds):

            @pl.when((start >= first) & (start < last))
            def _(source=source, first=first, start=start, index=index):
                pltpu.make_async_copy(
                    source.at[pl.ds(pl.multiple_of(start - first, size), size)],
                    raw.at[pl.ds(index * size, size)],
                    sems.at[index],
                ).start()

            first = last
    for index in range(starts.shape[-1]):
        pltpu.make_async_copy(
            sources[0].at[pl.ds(0, size)], raw.at[pl.ds(index * size, size)], sems.at[index]
        ).wait()
    stack[:depth], stack[depth:] = halves(raw[...])
    for at in range(cuts[0], cuts[-1], LANES):
        upto = min(at + LANES, cuts[-1])
        both = jnp.dot(stack[...], high_ref[:, at:upto], preferred_element_type=jnp.float32)
        rest = jnp.dot(stack[:depth], low_ref[:, at:upto], preferred_element_type=jnp.float32)
        total = both[:depth] + (both[depth:] + rest)
        for out_ref, left, right in zip(outs, cuts, cuts[1:]):
            first, last = max(at, left), min(upto, right)
            if first < last:
                out_ref[:, first - left : last - left] = total[:, first - at : last - at]


def product(sources, starts, size, pair, cuts):
    depth = starts.shape[-1] * size
    inner = pair[0].shape[0]
    width = cuts[-1] - cuts[0]
    return pl.pallas_call(
        functools.partial(product_kernel, starts, size, list(np.cumsum([s.shape[0] for s in sources])), cuts),
        out_shape=[jax.ShapeDtypeStruct((depth, right - left), jnp.float32) for left, right in zip(cuts, cuts[1:])],
        in_specs=[pl.BlockSpec(memory_space=pl.ANY)] * len(sources) + [pl.BlockSpec(memory_space=pltpu.VMEM)] * 2,
        out_specs=[pl.BlockSpec(memory_space=pltpu.VMEM)] * (len(cuts) - 1),
        scratch_shapes=[
            pltpu.VMEM((depth, inner), jnp.float32),
            pltpu.VMEM((2 * depth, inner), jnp.bfloat16),
            pltpu.SemaphoreType.DMA((starts.shape[-1],)),
        ],
        compiler_params=pltpu.CompilerParams(vmem_limit_bytes=16 * 2**20),
        cost_estimate=pl.CostEstimate(
            flops=6 * depth * inner * width,
            bytes_accessed=4 * depth * inner + 4 * inner * width + 4 * depth * width,
            transcendentals=0,
        ),
        name="product",
    )(*sources, *pair)


def finish_kernel(*refs):
    out_ref = refs[-1]
    for part in range(2):
        above, below, own = refs[3 * part : 3 * part + 3]
        width = own.shape[1]
        out_ref[:, part * width : (part + 1) * width] = (above[...] + below[...]) + own[...]


def finish(*values):
    depth, width = values[0].shape
    return pl.pallas_call(
        finish_kernel,
        out_shape=jax.ShapeDtypeStruct((depth, 2 * width), jnp.float32),
        in_specs=[pl.BlockSpec(memory_space=pltpu.VMEM)] * 6,
        out_specs=pl.BlockSpec(memory_space=pltpu.VMEM),
        compiler_params=pltpu.CompilerParams(vmem_limit_bytes=8 * 2**20),
        name="finish",
    )(*values)


def plan(order, rows, cols, size):
    place = np.zeros(rows, np.int64)
    place[order] = np.arange(rows)
    each, half = rows // cols, rows // 2
    steps = [half] + [way * (half - step) for step in range(1, half) for way in (1, -1)] + [0]
    taken = np.zeros((rows, cols, rows), np.int64)
    given = np.zeros((rows, cols, each), np.int64)
    for row in range(rows):
        needs = [order[(place[row] + step) % rows] for step in steps]
        for core in range(cols):
            arrived = 0
            for k, block in enumerate(needs):
                if block // each == core:
                    taken[row, core, k] = (block - core * each) * size
                else:
                    taken[row, core, k] = (each + arrived) * size
                    arrived += 1
            given[row, core] = [(block - core * each) * size for block in needs if block // each == core]
    return taken, given


def solution(mesh):
    rows, cols = mesh.shape["row"], mesh.shape["col"]
    order = ring_order(mesh)
    group = max(rows // CALLS, 1)
    half = rows // 2
    swap = [(core, cols - 1 - core) for core in range(cols)]
    ways = [[(order[i], order[(i + way) % rows]) for i in range(rows)] for way in (1, -1)]

    def shards(inductance, current_rates):
        size = inductance.shape[0] * cols // rows
        taken, given = plan(order, rows, cols, size)
        width = current_rates.shape[1]
        cuts = [0, width // 2, width]
        held = given.shape[-1]

        def swapped(first, *after):
            return lax.ppermute(pick(inductance, given[..., first : first + group], size, *after), "col", swap)

        sources = [inductance, swapped(0)]
        pair = split(current_rates)
        for first in range(group, held, group):
            sources.append(swapped(first, pair[0]))
        starts = taken[..., :group]
        calls = [[product(sources[:2], starts, size, pair, cuts[part : part + 2])[0] for part in range(2)]]

        def term(index, part):
            call, at = divmod(index, group)
            while len(calls) <= call:
                first = len(calls) * group
                have = sources[: 2 + len(calls)]
                calls.append(product(have, taken[..., first : first + group], size, pair, cuts))
            return calls[call][part][at * size : (at + 1) * size]

        sums = [[None, None], [None, None]]
        for step in range(half):
            for late in (1, 0):
                for way in range(2):
                    part = (way + late) % 2
                    if step == 0 and late:
                        continue
                    value = term(2 * step - 1 + way if step else 0, part)
                    if sums[way][part] is not None:
                        value = sums[way][part] + value
                    sums[way][part] = lax.ppermute(value, "row", ways[way])
        return finish(*(each for part in range(2) for each in (sums[0][part], sums[1][part], term(rows - 1, part))))

    placed = (P(("groups", "col"), "row"), P("row", ("groups", "col")))
    return jax.shard_map(
        shards, mesh=mesh, in_specs=placed, out_specs=P("row", ("groups", "col")), check_vma=False
    )
```

```python
import functools

import jax
import jax.numpy as jnp
import numpy as np
from jax import lax
from jax.experimental import pallas as pl
from jax.experimental.pallas import tpu as pltpu
from jax.sharding import PartitionSpec as P

CALLS = 8
LANES = 256
MIB = 2**20


def ring_order(mesh):
    count = mesh.shape["row"]
    axes = list(mesh.axis_names)
    line = np.moveaxis(mesh.devices, axes.index("row"), 0).reshape(count, -1)[:, 0]
    spots = [tuple(device.coords) for device in line]
    moving = [axis for axis in range(3) if len({spot[axis] for spot in spots}) > 1]
    plain = list(range(count))
    if len(moving) != 2:
        return plain
    for outer, inner in (moving, moving[::-1]):
        across = sorted({spot[outer] for spot in spots})
        along = sorted({spot[inner] for spot in spots})
        if len(across) % 2 or len(across) * len(along) != count:
            continue
        at = {(spot[outer], spot[inner]): index for index, spot in enumerate(spots)}
        walk = [at[across[0], along[0]]]
        for turn, a in enumerate(across):
            rest = along[1:]
            walk += [at[a, b] for b in (rest if turn % 2 == 0 else rest[::-1])]
        walk += [at[a, along[0]] for a in across[:0:-1]]
        return walk
    return plain


def looked_up(table):
    row, col = lax.axis_index("row"), lax.axis_index("col")
    found = jnp.int32(0)
    for r in range(table.shape[0]):
        for c in range(table.shape[1]):
            found = jnp.where((row == r) & (col == c), jnp.int32(table[r, c]), found)
    return found


def pick_kernel(starts, size, group, a_ref, *refs):
    count = starts.shape[-1]
    outs, sems = refs[-1 - count // group : -1], refs[-1]
    copies = []
    for index in range(count):
        start = pl.multiple_of(looked_up(starts[..., index]), size)
        out_ref, at = outs[index // group], index % group * size
        copies.append(
            pltpu.make_async_copy(
                a_ref.at[pl.ds(start, size)], out_ref.at[pl.ds(at, size)], sems.at[index]
            )
        )
    for copy in copies:
        copy.start()
    for copy in copies:
        copy.wait()


def pick(inductance, starts, size, group, room, *after):
    count = starts.shape[-1]
    width = inductance.shape[1]
    return pl.pallas_call(
        functools.partial(pick_kernel, starts, size, group),
        out_shape=[jax.ShapeDtypeStruct((group * size, width), jnp.float32)] * (count // group),
        in_specs=[pl.BlockSpec(memory_space=pl.ANY)] * (1 + len(after)),
        out_specs=[pl.BlockSpec(memory_space=pltpu.VMEM)] * (count // group),
        scratch_shapes=[pltpu.SemaphoreType.DMA((count,))],
        compiler_params=pltpu.CompilerParams(vmem_limit_bytes=room * MIB),
        cost_estimate=pl.CostEstimate(flops=0, bytes_accessed=8 * count * size * width, transcendentals=0),
        name="pick",
    )(inductance, *after)


def halves(value):
    high = value.astype(jnp.bfloat16)
    return high, (value - high.astype(jnp.float32)).astype(jnp.bfloat16)


def split_kernel(value_ref, high_ref, low_ref):
    high_ref[...], low_ref[...] = halves(value_ref[...])


def split(current_rates):
    depth, width = current_rates.shape
    tile = min(256, depth)
    out = jax.ShapeDtypeStruct((depth, width), jnp.bfloat16)
    return pl.pallas_call(
        split_kernel,
        grid=(depth // tile,),
        out_shape=(out, out),
        in_specs=[pl.BlockSpec((tile, width), lambda k: (k, 0))],
        out_specs=[pl.BlockSpec((tile, width), lambda k: (k, 0))] * 2,
        compiler_params=pltpu.CompilerParams(vmem_limit_bytes=8 * MIB),
        cost_estimate=pl.CostEstimate(flops=4 * depth * width, bytes_accessed=8 * depth * width, transcendentals=0),
        name="split",
    )(current_rates)


def product_kernel(starts, size, bounds, cuts, *refs):
    count = len(bounds)
    sources, (high_ref, low_ref), outs = refs[:count], refs[count : count + 2], refs[count + 2 : -3]
    raw, stack, sems = refs[-3:]
    depth = raw.shape[0]
    for index in range(starts.shape[-1]):
        start = looked_up(starts[..., index])
        first = 0
        for source, last in zip(sources, bounds):

            @pl.when((start >= first) & (start < last))
            def _(source=source, first=first, start=start, index=index):
                pltpu.make_async_copy(
                    source.at[pl.ds(pl.multiple_of(start - first, size), size)],
                    raw.at[pl.ds(index * size, size)],
                    sems.at[index],
                ).start()

            first = last
    for index in range(starts.shape[-1]):
        pltpu.make_async_copy(
            sources[0].at[pl.ds(0, size)], raw.at[pl.ds(index * size, size)], sems.at[index]
        ).wait()
    stack[:depth], stack[depth:] = halves(raw[...])
    for at in range(cuts[0], cuts[-1], LANES):
        upto = min(at + LANES, cuts[-1])
        both = jnp.dot(stack[...], high_ref[:, at:upto], preferred_element_type=jnp.float32)
        rest = jnp.dot(stack[:depth], low_ref[:, at:upto], preferred_element_type=jnp.float32)
        total = both[:depth] + (both[depth:] + rest)
        for out_ref, left, right in zip(outs, cuts, cuts[1:]):
            first, last = max(at, left), min(upto, right)
            if first < last:
                out_ref[:, first - left : last - left] = total[:, first - at : last - at]


def product(sources, starts, size, pair, cuts):
    depth = starts.shape[-1] * size
    inner = pair[0].shape[0]
    width = cuts[-1] - cuts[0]
    return pl.pallas_call(
        functools.partial(product_kernel, starts, size, list(np.cumsum([s.shape[0] for s in sources])), cuts),
        out_shape=[jax.ShapeDtypeStruct((depth, right - left), jnp.float32) for left, right in zip(cuts, cuts[1:])],
        in_specs=[pl.BlockSpec(memory_space=pl.ANY)] * len(sources) + [pl.BlockSpec(memory_space=pltpu.VMEM)] * 2,
        out_specs=[pl.BlockSpec(memory_space=pltpu.VMEM)] * (len(cuts) - 1),
        scratch_shapes=[
            pltpu.VMEM((depth, inner), jnp.float32),
            pltpu.VMEM((2 * depth, inner), jnp.bfloat16),
            pltpu.SemaphoreType.DMA((starts.shape[-1],)),
        ],
        compiler_params=pltpu.CompilerParams(vmem_limit_bytes=16 * MIB),
        cost_estimate=pl.CostEstimate(
            flops=6 * depth * inner * width,
            bytes_accessed=4 * depth * inner + 4 * inner * width + 4 * depth * width,
            transcendentals=0,
        ),
        name="product",
    )(*sources, *pair)


def finish_kernel(*refs):
    out_ref = refs[-1]
    for part in range(2):
        above, below, own = refs[3 * part : 3 * part + 3]
        width = own.shape[1]
        out_ref[:, part * width : (part + 1) * width] = (above[...] + below[...]) + own[...]


def finish(*values):
    depth, width = values[0].shape
    return pl.pallas_call(
        finish_kernel,
        out_shape=jax.ShapeDtypeStruct((depth, 2 * width), jnp.float32),
        in_specs=[pl.BlockSpec(memory_space=pltpu.VMEM)] * 6,
        out_specs=pl.BlockSpec(memory_space=pltpu.VMEM),
        compiler_params=pltpu.CompilerParams(vmem_limit_bytes=8 * MIB),
        name="finish",
    )(*values)


def plan(order, rows, cols, size, group):
    place = np.zeros(rows, np.int64)
    place[order] = np.arange(rows)
    each, half = rows // cols, rows // 2
    steps = [half] + [way * (half - step) for step in range(1, half) for way in (1, -1)] + [0]
    taken = np.zeros((rows, cols, rows), np.int64)
    given = np.zeros((rows, cols, each), np.int64)
    for row in range(rows):
        needs = [order[(place[row] + step) % rows] for step in steps]
        for core in range(cols):
            seen = [0, 0]
            for k, block in enumerate(needs):
                received = int(block // each != core)
                chunk, at = divmod(seen[received], group)
                taken[row, core, k] = ((2 * chunk + received) * group + at) * size
                seen[received] += 1
            given[row, core] = [(block - core * each) * size for block in needs if block // each == core]
    return taken, given


def solution(mesh):
    rows, cols = mesh.shape["row"], mesh.shape["col"]
    order = ring_order(mesh)
    group = max(rows // CALLS, 1)
    half = rows // 2
    swap = [(core, cols - 1 - core) for core in range(cols)]
    ways = [[(order[i], order[(i + way) % rows]) for i in range(rows)] for way in (1, -1)]

    def shards(inductance, current_rates):
        size = inductance.shape[0] * cols // rows
        taken, given = plan(order, rows, cols, size, group)
        width = current_rates.shape[1]
        cuts = [0, width // 2, width]
        calls = {}

        def term(index, part):
            call, at = divmod(index, group)
            if (call, part) not in calls:
                parts = [part] if call < 3 else [0, 1]
                starts = taken[..., call * group : (call + 1) * group]
                edges = cuts[parts[0] : parts[-1] + 2]
                got = product(sources[: 2 * call + 2], starts, size, pair, edges)
                calls.update({(call, each): value for each, value in zip(parts, got)})
            return calls[call, part][at * size : (at + 1) * size]

        own = pick(inductance, given[..., :group], size, group, 52)
        own += pick(inductance, given[..., group:], size, group, 48, *own)
        sources = [rows for each in own for rows in (each, lax.ppermute(each, "col", swap))]
        pair = split(current_rates)
        sums = [[None, None], [None, None]]
        for step in range(half):
            for late in (1, 0):
                for way in range(2):
                    part = (way + late) % 2
                    if step == 0 and late:
                        continue
                    value = term(2 * step - 1 + way if step else 0, part)
                    if sums[way][part] is not None:
                        value = sums[way][part] + value
                    sums[way][part] = lax.ppermute(value, "row", ways[way])
        return finish(*(each for part in range(2) for each in (sums[0][part], sums[1][part], term(rows - 1, part))))

    placed = (P(("groups", "col"), "row"), P("row", ("groups", "col")))
    return jax.shard_map(
        shards, mesh=mesh, in_specs=placed, out_specs=P("row", ("groups", "col")), check_vma=False
    )
```

```python
import functools

import jax
import jax.numpy as jnp
import numpy as np
from jax import lax
from jax.experimental import pallas as pl
from jax.experimental.pallas import tpu as pltpu
from jax.sharding import PartitionSpec as P

CALLS = 8
LANES = 256
MIB = 2**20


def ring_order(mesh):
    count = mesh.shape["row"]
    axes = list(mesh.axis_names)
    line = np.moveaxis(mesh.devices, axes.index("row"), 0).reshape(count, -1)[:, 0]
    spots = [tuple(device.coords) for device in line]
    moving = [axis for axis in range(3) if len({spot[axis] for spot in spots}) > 1]
    plain = list(range(count))
    if len(moving) != 2:
        return plain
    for outer, inner in (moving, moving[::-1]):
        across = sorted({spot[outer] for spot in spots})
        along = sorted({spot[inner] for spot in spots})
        if len(across) % 2 or len(across) * len(along) != count:
            continue
        at = {(spot[outer], spot[inner]): index for index, spot in enumerate(spots)}
        walk = [at[across[0], along[0]]]
        for turn, a in enumerate(across):
            rest = along[1:]
            walk += [at[a, b] for b in (rest if turn % 2 == 0 else rest[::-1])]
        walk += [at[a, along[0]] for a in across[:0:-1]]
        return walk
    return plain


def looked_up(table):
    row, col = lax.axis_index("row"), lax.axis_index("col")
    found = jnp.int32(0)
    for r in range(table.shape[0]):
        for c in range(table.shape[1]):
            found = jnp.where((row == r) & (col == c), jnp.int32(table[r, c]), found)
    return found


def block_copies(starts, size, chunks, a_ref, outs, sems):
    spots = [(out_ref, at * size) for out_ref, count in zip(outs, chunks) for at in range(count)]
    return [
        pltpu.make_async_copy(
            a_ref.at[pl.ds(pl.multiple_of(looked_up(starts[..., index]), size), size)],
            out_ref.at[pl.ds(at, size)],
            sems.at[index],
        )
        for index, (out_ref, at) in enumerate(spots)
    ]


def pick_kernel(starts, size, chunks, a_ref, out_ref, sems):
    copies = block_copies(starts, size, chunks, a_ref, [out_ref], sems)
    for copy in copies:
        copy.start()
    for copy in copies:
        copy.wait()


def pick(inductance, starts, size):
    count = starts.shape[-1]
    width = inductance.shape[1]
    return pl.pallas_call(
        functools.partial(pick_kernel, starts, size, [count]),
        out_shape=jax.ShapeDtypeStruct((count * size, width), jnp.float32),
        in_specs=[pl.BlockSpec(memory_space=pl.ANY)],
        out_specs=pl.BlockSpec(memory_space=pltpu.VMEM),
        scratch_shapes=[pltpu.SemaphoreType.DMA((count,))],
        compiler_params=pltpu.CompilerParams(vmem_limit_bytes=50 * MIB),
        cost_estimate=pl.CostEstimate(flops=0, bytes_accessed=8 * count * size * width, transcendentals=0),
        name="pick",
    )(inductance)


def first_column(part, width):
    return jnp.where((lax.axis_index("col") == 0) == (part == 0), width, 0)


def halves(value):
    high = value.astype(jnp.bfloat16)
    return high, (value - high.astype(jnp.float32)).astype(jnp.bfloat16)


def split_kernel(value_ref, high_ref, low_ref):
    high_ref[...], low_ref[...] = halves(value_ref[...])


def split(current_rates):
    depth, width = current_rates.shape
    tile = min(256, depth)
    tiled = pl.BlockSpec((tile, width), lambda k: (k, 0))
    return pl.pallas_call(
        split_kernel,
        grid=(depth // tile,),
        out_shape=[jax.ShapeDtypeStruct((depth, width), jnp.bfloat16)] * 2,
        in_specs=[tiled],
        out_specs=[tiled] * 2,
        compiler_params=pltpu.CompilerParams(vmem_limit_bytes=40 * MIB),
        cost_estimate=pl.CostEstimate(flops=4 * depth * width, bytes_accessed=8 * depth * width, transcendentals=0),
        name="split",
    )(current_rates)


def product_kernel(starts, size, bounds, parts, given, chunks, *refs):
    count = len(bounds)
    sources, (high_ref, low_ref), refs = refs[:count], refs[count : count + 2], refs[count + 2 :]
    *outs, raw, stack, sems, late_sems = refs
    depth = raw.shape[0]
    late = []
    if chunks:
        a_ref, *outs = outs
        late = block_copies(given, size, chunks, a_ref, outs[len(parts) :], late_sems)
    for copy in late:
        copy.start()
    for index in range(starts.shape[-1]):
        start = looked_up(starts[..., index])
        first = 0
        for source, last in zip(sources, bounds):

            @pl.when((start >= first) & (start < last))
            def _(source=source, first=first, start=start, index=index):
                pltpu.make_async_copy(
                    source.at[pl.ds(pl.multiple_of(start - first, size), size)],
                    raw.at[pl.ds(index * size, size)],
                    sems.at[index],
                ).start()

            first = last
    for index in range(starts.shape[-1]):
        pltpu.make_async_copy(
            sources[0].at[pl.ds(0, size)], raw.at[pl.ds(index * size, size)], sems.at[index]
        ).wait()
    stack[:depth], stack[depth:] = halves(raw[...])
    for part, out_ref in zip(parts, outs):
        width = out_ref.shape[1]
        tile = min(LANES, width)
        for at in range(0, width, tile):
            columns = pl.ds(pl.multiple_of(first_column(part, width) + at, tile), tile)
            both = jnp.dot(stack[...], high_ref[:, columns], preferred_element_type=jnp.float32)
            rest = jnp.dot(stack[:depth], low_ref[:, columns], preferred_element_type=jnp.float32)
            out_ref[:, at : at + tile] = both[:depth] + (both[depth:] + rest)
    for copy in late:
        copy.wait()


def product(sources, starts, size, pair, parts, inductance=None, given=np.zeros(0), chunks=()):
    depth = starts.shape[-1] * size
    inner, width = pair[0].shape
    wanted = [inductance] if chunks else []
    half = jax.ShapeDtypeStruct((depth, width // 2), jnp.float32)
    return pl.pallas_call(
        functools.partial(
            product_kernel, starts, size, list(np.cumsum([s.shape[0] for s in sources])), parts, given, chunks
        ),
        out_shape=[half] * len(parts) + [jax.ShapeDtypeStruct((chunk * size, inner), jnp.float32) for chunk in chunks],
        in_specs=[pl.BlockSpec(memory_space=pl.ANY)] * len(sources) + [pl.BlockSpec(memory_space=pltpu.VMEM)] * 2
        + [pl.BlockSpec(memory_space=pl.ANY)] * len(wanted),
        out_specs=[pl.BlockSpec(memory_space=pltpu.VMEM)] * len(parts)
        + [pl.BlockSpec(memory_space=pl.ANY)] * len(chunks),
        scratch_shapes=[
            pltpu.VMEM((depth, inner), jnp.float32),
            pltpu.VMEM((2 * depth, inner), jnp.bfloat16),
            pltpu.SemaphoreType.DMA((starts.shape[-1],)),
            pltpu.SemaphoreType.DMA((max(given.shape[-1], 1),)),
        ],
        compiler_params=pltpu.CompilerParams(vmem_limit_bytes=(40 if chunks else 16) * MIB),
        cost_estimate=pl.CostEstimate(
            flops=3 * depth * inner * width * len(parts),
            bytes_accessed=4 * depth * inner + (2 * inner + 2 * depth) * width * len(parts),
            transcendentals=0,
        ),
        name="product",
    )(*sources, *pair, *wanted)


def finish_kernel(*refs):
    out_ref = refs[-1]
    for part in range(2):
        above, below, own = refs[3 * part : 3 * part + 3]
        width = own.shape[1]
        columns = pl.ds(pl.multiple_of(first_column(part, width), width), width)
        out_ref[:, columns] = (above[...] + below[...]) + own[...]


def finish(*values):
    depth, width = values[0].shape
    return pl.pallas_call(
        finish_kernel,
        out_shape=jax.ShapeDtypeStruct((depth, 2 * width), jnp.float32),
        in_specs=[pl.BlockSpec(memory_space=pltpu.VMEM)] * 6,
        out_specs=pl.BlockSpec(memory_space=pltpu.VMEM),
        compiler_params=pltpu.CompilerParams(vmem_limit_bytes=8 * MIB),
        name="finish",
    )(*values)


def plan(order, rows, cols, size, chunks):
    place = np.zeros(rows, np.int64)
    place[order] = np.arange(rows)
    each, half = rows // cols, rows // 2
    needs = np.zeros((rows, cols, rows), np.int64)
    for core in range(cols):
        ways = (-1, 1) if core == 0 else (1, -1)
        steps = [half] + [way * (half - step) for step in range(1, half) for way in ways] + [0]
        for row in range(rows):
            needs[row, core] = [order[(place[row] + step) % rows] for step in steps]
    spots = [(2 * sum(chunks[:chunk]) + at, count) for chunk, count in enumerate(chunks) for at in range(count)]
    taken = np.zeros((rows, cols, rows), np.int64)
    given = np.zeros((rows, cols, each), np.int64)
    for row in range(rows):
        for core in range(cols):
            sent = [block for block in needs[row, cols - 1 - core] if block // each == core]
            given[row, core] = [(block - core * each) * size for block in sent]
            arrived = 0
            for k, block in enumerate(needs[row, core]):
                if block // each == core:
                    taken[row, core, k] = spots[sent.index(block)][0] * size
                else:
                    taken[row, core, k] = sum(spots[arrived]) * size
                    arrived += 1
    return taken, given


def solution(mesh):
    rows, cols = mesh.shape["row"], mesh.shape["col"]
    order = ring_order(mesh)
    group = max(rows // CALLS, 1)
    half = rows // 2
    swap = [(core, cols - 1 - core) for core in range(cols)]
    ways = [
        [
            (order[i] * cols + core, order[(i + (way if core else -way)) % rows] * cols + core)
            for i in range(rows)
            for core in range(cols)
        ]
        for way in (1, -1)
    ]

    def shards(inductance, current_rates):
        size = inductance.shape[0] * cols // rows
        spare = int(group > 1)
        chunks = [group + spare] + [group] * (rows // cols // group - 2) + [group - spare]
        taken, given = plan(order, rows, cols, size, chunks)
        own = [pick(inductance, given[..., : chunks[0]], size)]
        received = [lax.ppermute(own[0], "col", swap)]
        pair = split(current_rates)
        early, *later = product(
            [own[0], received[0]], taken[..., :group], size, pair, [0], inductance, given[..., chunks[0] :], chunks[1:]
        )
        own += later
        received += [lax.ppermute(each, "col", swap) for each in later]
        sources = [rows for pair_of in zip(own, received) for rows in pair_of]
        firsts = np.cumsum([0] + [each.shape[0] for each in sources])
        calls = {(0, 0): early}

        def term(index, part):
            call, at = divmod(index, group)
            if (call, part) not in calls:
                parts = [part] if call < 3 else [0, 1]
                starts = taken[..., call * group : (call + 1) * group]
                have = sources[: int(np.searchsorted(firsts, starts.max(), "right"))]
                got = product(have, starts, size, pair, parts)
                calls.update({(call, each): value for each, value in zip(parts, got)})
            return calls[call, part][at * size : (at + 1) * size]

        sums = [[None, None], [None, None]]
        for step in range(half):
            for late in (1, 0):
                for way in range(2):
                    part = (way + late) % 2
                    if step == 0 and late:
                        continue
                    value = term(2 * step - 1 + way if step else 0, part)
                    if sums[way][part] is not None:
                        value = sums[way][part] + value
                    sums[way][part] = lax.ppermute(value, ("row", "col"), ways[way])
        return finish(*(each for part in range(2) for each in (sums[0][part], sums[1][part], term(rows - 1, part))))

    placed = (P(("groups", "col"), "row"), P("row", ("groups", "col")))
    return jax.shard_map(
        shards, mesh=mesh, in_specs=placed, out_specs=P("row", ("groups", "col")), check_vma=False
    )
```

```python
import functools

import jax
import jax.numpy as jnp
import numpy as np
from jax import lax
from jax.experimental import pallas as pl
from jax.experimental.pallas import tpu as pltpu
from jax.sharding import PartitionSpec as P

CALLS = 8
LANES = 256
PIECE = 16
MIB = 2**20


def ring_order(mesh):
    count = mesh.shape["row"]
    axes = list(mesh.axis_names)
    line = np.moveaxis(mesh.devices, axes.index("row"), 0).reshape(count, -1)[:, 0]
    spots = [tuple(device.coords) for device in line]
    moving = [axis for axis in range(3) if len({spot[axis] for spot in spots}) > 1]
    plain = list(range(count))
    if len(moving) != 2:
        return plain
    for outer, inner in (moving, moving[::-1]):
        across = sorted({spot[outer] for spot in spots})
        along = sorted({spot[inner] for spot in spots})
        if len(across) % 2 or len(across) * len(along) != count:
            continue
        at = {(spot[outer], spot[inner]): index for index, spot in enumerate(spots)}
        walk = [at[across[0], along[0]]]
        for turn, a in enumerate(across):
            rest = along[1:]
            walk += [at[a, b] for b in (rest if turn % 2 == 0 else rest[::-1])]
        walk += [at[a, along[0]] for a in across[:0:-1]]
        return walk
    return plain


def looked_up(table):
    row, col = lax.axis_index("row"), lax.axis_index("col")
    found = jnp.int32(0)
    for r in range(table.shape[0]):
        for c in range(table.shape[1]):
            found = jnp.where((row == r) & (col == c), jnp.int32(table[r, c]), found)
    return found


def pick_kernel(starts, size, chunks, a_ref, *refs):
    outs, sems = refs[-1 - len(chunks) : -1], refs[-1]
    spots = [(chunk, at * size) for chunk, count in enumerate(chunks) for at in range(count)]
    piece = min(size, PIECE)
    for index, (chunk, first) in enumerate(spots):
        start = looked_up(starts[..., index])
        for at in range(0, size, piece):
            pltpu.make_async_copy(
                a_ref.at[pl.ds(pl.multiple_of(start + at, piece), piece)],
                outs[chunk].at[pl.ds(first + at, piece)],
                sems.at[chunk],
            ).start()
    for chunk, out_ref in enumerate(outs):
        pltpu.make_async_copy(a_ref.at[pl.ds(0, out_ref.shape[0])], out_ref, sems.at[chunk]).wait()


def pick(inductance, starts, size, chunks, room, *after):
    width = inductance.shape[1]
    moved = 8 * sum(chunks) * size * width
    return pl.pallas_call(
        functools.partial(pick_kernel, starts, size, chunks),
        out_shape=[jax.ShapeDtypeStruct((count * size, width), jnp.float32) for count in chunks],
        in_specs=[pl.BlockSpec(memory_space=pl.ANY)] * (1 + len(after)),
        out_specs=[pl.BlockSpec(memory_space=pltpu.VMEM)] * len(chunks),
        scratch_shapes=[pltpu.SemaphoreType.DMA((len(chunks),))],
        compiler_params=pltpu.CompilerParams(vmem_limit_bytes=room * MIB),
        cost_estimate=pl.CostEstimate(flops=0, bytes_accessed=moved, transcendentals=0),
        name="pick",
    )(inductance, *after)


def side(part):
    return jnp.where((lax.axis_index("col") == 0) == (part == 0), 1, 0)


def halves(value):
    high = value.astype(jnp.bfloat16)
    return high, (value - high.astype(jnp.float32)).astype(jnp.bfloat16)


def split_kernel(value_ref, *refs):
    high_ref, low_ref = refs[-2:]
    high_ref[...], low_ref[...] = halves(value_ref[...])


def split(current_rates, part, *after):
    depth, width = current_rates.shape
    width //= 2
    tile = min(512, depth)
    return pl.pallas_call(
        split_kernel,
        grid=(depth // tile,),
        out_shape=[jax.ShapeDtypeStruct((depth, width), jnp.bfloat16)] * 2,
        in_specs=[pl.BlockSpec((tile, width), lambda k: (k, side(part)))]
        + [pl.BlockSpec(memory_space=pl.ANY)] * len(after),
        out_specs=[pl.BlockSpec((tile, width), lambda k: (k, 0))] * 2,
        compiler_params=pltpu.CompilerParams(vmem_limit_bytes=8 * MIB),
        cost_estimate=pl.CostEstimate(flops=4 * depth * width, bytes_accessed=8 * depth * width, transcendentals=0),
        name="split",
    )(current_rates, *after)


def product_kernel(starts, size, bounds, parts, *refs):
    count = len(bounds)
    sources, pairs = refs[:count], refs[count : count + 2 * parts]
    outs, (raw, stack, sems) = refs[-3 - parts : -3], refs[-3:]
    depth = raw.shape[0]
    for index in range(starts.shape[-1]):
        start = looked_up(starts[..., index])
        first = 0
        for source, last in zip(sources, bounds):

            @pl.when((start >= first) & (start < last))
            def _(source=source, first=first, start=start, index=index):
                pltpu.make_async_copy(
                    source.at[pl.ds(pl.multiple_of(start - first, size), size)],
                    raw.at[pl.ds(index * size, size)],
                    sems.at[index],
                ).start()

            first = last
    for index in range(starts.shape[-1]):
        pltpu.make_async_copy(
            sources[0].at[pl.ds(0, size)], raw.at[pl.ds(index * size, size)], sems.at[index]
        ).wait()
    stack[:depth], stack[depth:] = halves(raw[...])
    for part, out_ref in enumerate(outs):
        high_ref, low_ref = pairs[2 * part : 2 * part + 2]
        width = out_ref.shape[1]
        tile = min(LANES, width)
        for at in range(0, width, tile):
            both = jnp.dot(stack[...], high_ref[:, at : at + tile], preferred_element_type=jnp.float32)
            rest = jnp.dot(stack[:depth], low_ref[:, at : at + tile], preferred_element_type=jnp.float32)
            out_ref[:, at : at + tile] = both[:depth] + (both[depth:] + rest)


def product(sources, starts, size, pairs, *after):
    depth = starts.shape[-1] * size
    inner, width = pairs[0].shape
    parts = len(pairs) // 2
    anywhere, whole = pl.BlockSpec(memory_space=pl.ANY), pl.BlockSpec(memory_space=pltpu.VMEM)
    return pl.pallas_call(
        functools.partial(product_kernel, starts, size, list(np.cumsum([s.shape[0] for s in sources])), parts),
        out_shape=[jax.ShapeDtypeStruct((depth, width), jnp.float32)] * parts,
        in_specs=[anywhere] * len(sources) + [whole] * len(pairs) + [anywhere] * len(after),
        out_specs=[whole] * parts,
        scratch_shapes=[
            pltpu.VMEM((depth, inner), jnp.float32),
            pltpu.VMEM((2 * depth, inner), jnp.bfloat16),
            pltpu.SemaphoreType.DMA((starts.shape[-1],)),
        ],
        compiler_params=pltpu.CompilerParams(vmem_limit_bytes=16 * MIB),
        cost_estimate=pl.CostEstimate(
            flops=6 * depth * inner * width * parts,
            bytes_accessed=4 * depth * inner + 4 * (inner + depth) * width * parts,
            transcendentals=0,
        ),
        name="product",
    )(*sources, *pairs, *after)


def finish_kernel(*refs):
    out_ref = refs[-1]
    for part in range(2):
        above, below, own = refs[3 * part : 3 * part + 3]
        width = own.shape[1]
        columns = pl.ds(pl.multiple_of(side(part) * width, width), width)
        out_ref[:, columns] = (above[...] + below[...]) + own[...]


def finish(*values):
    depth, width = values[0].shape
    return pl.pallas_call(
        finish_kernel,
        out_shape=jax.ShapeDtypeStruct((depth, 2 * width), jnp.float32),
        in_specs=[pl.BlockSpec(memory_space=pltpu.VMEM)] * 6,
        out_specs=pl.BlockSpec(memory_space=pltpu.VMEM),
        compiler_params=pltpu.CompilerParams(vmem_limit_bytes=8 * MIB),
        name="finish",
    )(*values)


def plan(order, rows, cols, size, chunks):
    place = np.zeros(rows, np.int64)
    place[order] = np.arange(rows)
    each, half = rows // cols, rows // 2
    needs = np.zeros((rows, cols, rows), np.int64)
    for core in range(cols):
        ways = (-1, 1) if core == 0 else (1, -1)
        steps = [half] + [way * (half - step) for step in range(1, half) for way in ways] + [0]
        for row in range(rows):
            needs[row, core] = [order[(place[row] + step) % rows] for step in steps]
    spots = [(2 * sum(chunks[:chunk]) + at, count) for chunk, count in enumerate(chunks) for at in range(count)]
    taken = np.zeros((rows, cols, rows), np.int64)
    given = np.zeros((rows, cols, each), np.int64)
    for row in range(rows):
        for core in range(cols):
            sent = [block for block in needs[row, cols - 1 - core] if block // each == core]
            given[row, core] = [(block - core * each) * size for block in sent]
            arrived = 0
            for k, block in enumerate(needs[row, core]):
                if block // each == core:
                    taken[row, core, k] = spots[sent.index(block)][0] * size
                else:
                    taken[row, core, k] = sum(spots[arrived]) * size
                    arrived += 1
    return taken, given


def solution(mesh):
    rows, cols = mesh.shape["row"], mesh.shape["col"]
    order = ring_order(mesh)
    group = max(rows // CALLS, 1)
    half = rows // 2
    swap = [(core, cols - 1 - core) for core in range(cols)]
    ways = [
        [
            (order[i] * cols + core, order[(i + (way if core else -way)) % rows] * cols + core)
            for i in range(rows)
            for core in range(cols)
        ]
        for way in (1, -1)
    ]

    def shards(inductance, current_rates):
        size = inductance.shape[0] * cols // rows
        spare = int(group > 1)
        chunks = [group + spare] + [group] * (rows // cols // group - 2) + [group - spare]
        taken, given = plan(order, rows, cols, size, chunks)
        own = pick(inductance, given[..., : chunks[0]], size, chunks[:1], 52)
        own += pick(inductance, given[..., chunks[0] :], size, chunks[1:], 48, *own)
        received = [lax.ppermute(each, "col", swap) for each in own]
        sources = [rows for pair in zip(own, received) for rows in pair]
        firsts = np.cumsum([0] + [each.shape[0] for each in sources])
        pairs, calls, made = {}, {}, []

        def term(index, part):
            call, at = divmod(index, group)
            if (call, part) not in calls:
                parts = [part] if call < 3 else [0, 1]
                for each in parts:
                    if each not in pairs:
                        pairs[each] = split(current_rates, each, *made)
                starts = taken[..., call * group : (call + 1) * group]
                have = sources[: int(np.searchsorted(firsts, starts.max(), "right"))]
                got = product(have, starts, size, [half for each in parts for half in pairs[each]], *made[-1:])
                calls.update({(call, each): value for each, value in zip(parts, got)})
                made.append(got[0])
            return calls[call, part][at * size : (at + 1) * size]

        sums = [[None, None], [None, None]]
        for step in range(half):
            for late in (1, 0):
                for way in range(2):
                    part = (way + late) % 2
                    if step == 0 and late:
                        continue
                    value = term(2 * step - 1 + way if step else 0, part)
                    if sums[way][part] is not None:
                        value = sums[way][part] + value
                    sums[way][part] = lax.ppermute(value, ("row", "col"), ways[way])
        return finish(*(each for part in range(2) for each in (sums[0][part], sums[1][part], term(rows - 1, part))))

    placed = (P(("groups", "col"), "row"), P("row", ("groups", "col")))
    return jax.shard_map(
        shards, mesh=mesh, in_specs=placed, out_specs=P("row", ("groups", "col")), check_vma=False
    )
```

```python
import functools

import jax
import jax.numpy as jnp
import numpy as np
from jax import lax
from jax.experimental import pallas as pl
from jax.experimental.pallas import tpu as pltpu
from jax.sharding import PartitionSpec as P

CALLS = 8
LANES = 256
PIECE = 16
MIB = 2**20


def ring_order(mesh):
    count = mesh.shape["row"]
    axes = list(mesh.axis_names)
    line = np.moveaxis(mesh.devices, axes.index("row"), 0).reshape(count, -1)[:, 0]
    spots = [tuple(device.coords) for device in line]
    moving = [axis for axis in range(3) if len({spot[axis] for spot in spots}) > 1]
    plain = list(range(count))
    if len(moving) != 2:
        return plain
    for outer, inner in (moving, moving[::-1]):
        across = sorted({spot[outer] for spot in spots})
        along = sorted({spot[inner] for spot in spots})
        if len(across) % 2 or len(across) * len(along) != count:
            continue
        at = {(spot[outer], spot[inner]): index for index, spot in enumerate(spots)}
        walk = [at[across[0], along[0]]]
        for turn, a in enumerate(across):
            rest = along[1:]
            walk += [at[a, b] for b in (rest if turn % 2 == 0 else rest[::-1])]
        walk += [at[a, along[0]] for a in across[:0:-1]]
        return walk
    return plain


def looked_up(table):
    row, col = lax.axis_index("row"), lax.axis_index("col")
    found = jnp.int32(0)
    for r in range(table.shape[0]):
        for c in range(table.shape[1]):
            found = jnp.where((row == r) & (col == c), jnp.int32(table[r, c]), found)
    return found


def pick_kernel(starts, size, chunks, a_ref, *refs):
    outs, sems = refs[-1 - len(chunks) : -1], refs[-1]
    spots = [(chunk, at * size) for chunk, count in enumerate(chunks) for at in range(count)]
    piece = min(size, PIECE)
    for index, (chunk, first) in enumerate(spots):
        start = looked_up(starts[..., index])
        for at in range(0, size, piece):
            pltpu.make_async_copy(
                a_ref.at[pl.ds(pl.multiple_of(start + at, piece), piece)],
                outs[chunk].at[pl.ds(first + at, piece)],
                sems.at[chunk],
            ).start()
    for chunk, out_ref in enumerate(outs):
        pltpu.make_async_copy(a_ref.at[pl.ds(0, out_ref.shape[0])], out_ref, sems.at[chunk]).wait()


def pick(inductance, starts, size, chunks, room, *after):
    width = inductance.shape[1]
    moved = 8 * sum(chunks) * size * width
    return pl.pallas_call(
        functools.partial(pick_kernel, starts, size, chunks),
        out_shape=[jax.ShapeDtypeStruct((count * size, width), jnp.float32) for count in chunks],
        in_specs=[pl.BlockSpec(memory_space=pl.ANY)] * (1 + len(after)),
        out_specs=[pl.BlockSpec(memory_space=pltpu.VMEM)] * len(chunks),
        scratch_shapes=[pltpu.SemaphoreType.DMA((len(chunks),))],
        compiler_params=pltpu.CompilerParams(vmem_limit_bytes=room * MIB),
        cost_estimate=pl.CostEstimate(flops=0, bytes_accessed=moved, transcendentals=0),
        name="pick",
    )(inductance, *after)


def side(part):
    return jnp.where((lax.axis_index("col") == 0) == (part == 0), 1, 0)


def halves(value):
    high = value.astype(jnp.bfloat16)
    return high, (value - high.astype(jnp.float32)).astype(jnp.bfloat16)


def split_kernel(value_ref, *refs):
    high_ref, low_ref = refs[-2:]
    high_ref[...], low_ref[...] = halves(value_ref[...])


def split(current_rates, part, *after):
    depth, width = current_rates.shape
    width //= 2
    tile = min(512, depth)
    return pl.pallas_call(
        split_kernel,
        grid=(depth // tile,),
        out_shape=[jax.ShapeDtypeStruct((depth, width), jnp.bfloat16)] * 2,
        in_specs=[pl.BlockSpec((tile, width), lambda k: (k, side(part)))]
        + [pl.BlockSpec(memory_space=pl.ANY)] * len(after),
        out_specs=[pl.BlockSpec((tile, width), lambda k: (k, 0))] * 2,
        compiler_params=pltpu.CompilerParams(vmem_limit_bytes=8 * MIB),
        cost_estimate=pl.CostEstimate(flops=4 * depth * width, bytes_accessed=8 * depth * width, transcendentals=0),
        name="split",
    )(current_rates, *after)


def product_kernel(starts, size, bounds, parts, *refs):
    count = len(bounds)
    sources, pairs = refs[:count], refs[count : count + 2 * parts]
    if starts is None:
        (stack,), outs = sources, refs[-parts:]
        depth = stack.shape[0] // 2
    else:
        outs, (stack, raw, sems) = refs[-3 - parts : -3], refs[-3:]
        depth = raw.shape[0]
        for index in range(starts.shape[-1]):
            start = looked_up(starts[..., index])
            first = 0
            for source, last in zip(sources, bounds):

                @pl.when((start >= first) & (start < last))
                def _(source=source, first=first, start=start, index=index):
                    pltpu.make_async_copy(
                        source.at[pl.ds(pl.multiple_of(start - first, size), size)],
                        raw.at[pl.ds(index * size, size)],
                        sems.at[index],
                    ).start()

                first = last
        for index in range(starts.shape[-1]):
            pltpu.make_async_copy(
                sources[0].at[pl.ds(0, size)], raw.at[pl.ds(index * size, size)], sems.at[index]
            ).wait()
        stack[:depth], stack[depth:] = halves(raw[...])
    for part, out_ref in enumerate(outs):
        high_ref, low_ref = pairs[2 * part : 2 * part + 2]
        width = out_ref.shape[1]
        tile = min(LANES, width)
        for at in range(0, width, tile):
            both = jnp.dot(stack[...], high_ref[:, at : at + tile], preferred_element_type=jnp.float32)
            rest = jnp.dot(stack[:depth], low_ref[:, at : at + tile], preferred_element_type=jnp.float32)
            out_ref[:, at : at + tile] = both[:depth] + (both[depth:] + rest)


def product(sources, starts, size, pairs, *after):
    again = starts is None
    depth = sources[0].shape[0] // 2 if again else starts.shape[-1] * size
    inner, width = pairs[0].shape
    parts = len(pairs) // 2
    anywhere, whole = pl.BlockSpec(memory_space=pl.ANY), pl.BlockSpec(memory_space=pltpu.VMEM)
    fetch = [pltpu.VMEM((depth, inner), jnp.float32)]
    fetch += [] if again else [pltpu.SemaphoreType.DMA((starts.shape[-1],))]
    got = pl.pallas_call(
        functools.partial(product_kernel, starts, size, list(np.cumsum([s.shape[0] for s in sources])), parts),
        out_shape=[jax.ShapeDtypeStruct((depth, width), jnp.float32)] * parts
        + [jax.ShapeDtypeStruct((2 * depth, inner), jnp.bfloat16)] * (not again),
        in_specs=[whole if again else anywhere] * len(sources) + [whole] * len(pairs) + [anywhere] * len(after),
        out_specs=[whole] * (parts + (not again)),
        scratch_shapes=[] if again else fetch,
        compiler_params=pltpu.CompilerParams(vmem_limit_bytes=16 * MIB),
        cost_estimate=pl.CostEstimate(
            flops=6 * depth * inner * width * parts,
            bytes_accessed=4 * depth * inner + 4 * (inner + depth) * width * parts,
            transcendentals=0,
        ),
        name="product",
    )(*sources, *pairs, *after)
    return [*got, sources[0]] if again else got


def finish_kernel(*refs):
    out_ref, total, sems = refs[-3:]
    rows = total.shape[0] // sems.shape[0]
    copies = []
    for index in range(sems.shape[0]):
        at = slice(index * rows, (index + 1) * rows)
        for part in range(2):
            above, below, own = refs[3 * part : 3 * part + 3]
            width = own.shape[1]
            columns = pl.ds(pl.multiple_of(side(part) * width, width), width)
            total[at, columns] = (above[at] + below[at]) + own[at]
        copies.append(pltpu.make_async_copy(total.at[at], out_ref.at[at], sems.at[index]))
        copies[-1].start()
    for copy in copies:
        copy.wait()


def finish(*values):
    depth, width = values[0].shape
    return pl.pallas_call(
        finish_kernel,
        out_shape=jax.ShapeDtypeStruct((depth, 2 * width), jnp.float32),
        in_specs=[pl.BlockSpec(memory_space=pltpu.VMEM)] * 6,
        out_specs=pl.BlockSpec(memory_space=pl.ANY),
        scratch_shapes=[
            pltpu.VMEM((depth, 2 * width), jnp.float32),
            pltpu.SemaphoreType.DMA((max(depth // PIECE, 1),)),
        ],
        compiler_params=pltpu.CompilerParams(vmem_limit_bytes=8 * MIB),
        name="finish",
    )(*values)


def plan(order, rows, cols, size, chunks):
    place = np.zeros(rows, np.int64)
    place[order] = np.arange(rows)
    each, half = rows // cols, rows // 2
    needs = np.zeros((rows, cols, rows), np.int64)
    for core in range(cols):
        ways = (-1, 1) if core == 0 else (1, -1)
        steps = [half] + [way * (half - step) for step in range(1, half) for way in ways] + [0]
        for row in range(rows):
            needs[row, core] = [order[(place[row] + step) % rows] for step in steps]
    spots = [(2 * sum(chunks[:chunk]) + at, count) for chunk, count in enumerate(chunks) for at in range(count)]
    taken = np.zeros((rows, cols, rows), np.int64)
    given = np.zeros((rows, cols, each), np.int64)
    for row in range(rows):
        for core in range(cols):
            sent = [block for block in needs[row, cols - 1 - core] if block // each == core]
            given[row, core] = [(block - core * each) * size for block in sent]
            arrived = 0
            for k, block in enumerate(needs[row, core]):
                if block // each == core:
                    taken[row, core, k] = spots[sent.index(block)][0] * size
                else:
                    taken[row, core, k] = sum(spots[arrived]) * size
                    arrived += 1
    return taken, given


def solution(mesh):
    rows, cols = mesh.shape["row"], mesh.shape["col"]
    order = ring_order(mesh)
    group = max(rows // CALLS, 1)
    half = rows // 2
    swap = [(core, cols - 1 - core) for core in range(cols)]
    ways = [
        [
            (order[i] * cols + core, order[(i + (way if core else -way)) % rows] * cols + core)
            for i in range(rows)
            for core in range(cols)
        ]
        for way in (1, -1)
    ]

    def shards(inductance, current_rates):
        size = inductance.shape[0] * cols // rows
        spare = int(group > 1)
        chunks = [group + spare] + [group] * (rows // cols // group - 2) + [group - spare]
        taken, given = plan(order, rows, cols, size, chunks)
        sources, pairs, calls, stacks, made = [], {}, {}, {}, []

        def fetch(first, last, room, *after):
            wanted = slice(sum(chunks[:first]), sum(chunks[:last]))
            for own in pick(inductance, given[..., wanted], size, chunks[first:last], room, *after):
                sources.extend([own, lax.ppermute(own, "col", swap)])

        def term(index, part):
            call, at = divmod(index, group)
            if (call, part) not in calls:
                parts = [part] if call < 3 else [0, 1]
                for each in parts:
                    if each not in pairs:
                        pairs[each] = split(current_rates, each, *made)
                starts = taken[..., call * group : (call + 1) * group]
                firsts = np.cumsum([0] + [each.shape[0] for each in sources])
                have = sources[: int(np.searchsorted(firsts, starts.max(), "right"))]
                if call in stacks:
                    have, starts = [stacks[call]], None
                *got, stacks[call] = product(
                    have, starts, size, [half for each in parts for half in pairs[each]], *made[-1:]
                )
                calls.update({(call, each): value for each, value in zip(parts, got)})
                made.append(got[0])
            return calls[call, part][at * size : (at + 1) * size]

        fetch(0, 1, 52)
        fetch(1, len(chunks), 48, sources[0])

        sums = [[None, None], [None, None]]
        for step in range(half):
            for late in (1, 0):
                for way in range(2):
                    part = (way + late) % 2
                    if step == 0 and late:
                        continue
                    value = term(2 * step - 1 + way if step else 0, part)
                    if sums[way][part] is not None:
                        value = sums[way][part] + value
                    sums[way][part] = lax.ppermute(value, ("row", "col"), ways[way])
        return finish(*(each for part in range(2) for each in (sums[0][part], sums[1][part], term(rows - 1, part))))

    placed = (P(("groups", "col"), "row"), P("row", ("groups", "col")))
    return jax.shard_map(
        shards, mesh=mesh, in_specs=placed, out_specs=P("row", ("groups", "col")), check_vma=False
    )
```

```python
import functools

import jax
import jax.numpy as jnp
import numpy as np
from jax import lax
from jax.experimental import pallas as pl
from jax.experimental.pallas import tpu as pltpu
from jax.sharding import PartitionSpec as P

CALLS = 8
LANES = 256
PIECE = 16
MIB = 2**20


def ring_order(mesh):
    count = mesh.shape["row"]
    axes = list(mesh.axis_names)
    line = np.moveaxis(mesh.devices, axes.index("row"), 0).reshape(count, -1)[:, 0]
    spots = [tuple(device.coords) for device in line]
    moving = [axis for axis in range(3) if len({spot[axis] for spot in spots}) > 1]
    plain = list(range(count))
    if len(moving) != 2:
        return plain
    for outer, inner in (moving, moving[::-1]):
        across = sorted({spot[outer] for spot in spots})
        along = sorted({spot[inner] for spot in spots})
        if len(across) % 2 or len(across) * len(along) != count:
            continue
        at = {(spot[outer], spot[inner]): index for index, spot in enumerate(spots)}
        walk = [at[across[0], along[0]]]
        for turn, a in enumerate(across):
            rest = along[1:]
            walk += [at[a, b] for b in (rest if turn % 2 == 0 else rest[::-1])]
        walk += [at[a, along[0]] for a in across[:0:-1]]
        return walk
    return plain


def looked_up(table):
    row, col = lax.axis_index("row"), lax.axis_index("col")
    found = jnp.int32(0)
    for r in range(table.shape[0]):
        for c in range(table.shape[1]):
            found = jnp.where((row == r) & (col == c), jnp.int32(table[r, c]), found)
    return found


def pick_kernel(starts, size, chunks, a_ref, *refs):
    outs, sems = refs[-1 - len(chunks) : -1], refs[-1]
    spots = [(chunk, at * size) for chunk, count in enumerate(chunks) for at in range(count)]
    piece = min(size, PIECE)
    for index, (chunk, first) in enumerate(spots):
        start = looked_up(starts[..., index])
        for at in range(0, size, piece):
            pltpu.make_async_copy(
                a_ref.at[pl.ds(pl.multiple_of(start + at, piece), piece)],
                outs[chunk].at[pl.ds(first + at, piece)],
                sems.at[chunk],
            ).start()
    for chunk, out_ref in enumerate(outs):
        pltpu.make_async_copy(a_ref.at[pl.ds(0, out_ref.shape[0])], out_ref, sems.at[chunk]).wait()


def pick(inductance, starts, size, chunks, room, *after):
    width = inductance.shape[1]
    moved = 8 * sum(chunks) * size * width
    return pl.pallas_call(
        functools.partial(pick_kernel, starts, size, chunks),
        out_shape=[jax.ShapeDtypeStruct((count * size, width), jnp.float32) for count in chunks],
        in_specs=[pl.BlockSpec(memory_space=pl.ANY)] * (1 + len(after)),
        out_specs=[pl.BlockSpec(memory_space=pltpu.VMEM)] * len(chunks),
        scratch_shapes=[pltpu.SemaphoreType.DMA((len(chunks),))],
        compiler_params=pltpu.CompilerParams(vmem_limit_bytes=room * MIB),
        cost_estimate=pl.CostEstimate(flops=0, bytes_accessed=moved, transcendentals=0),
        name="pick",
    )(inductance, *after)


def side(part):
    return jnp.where((lax.axis_index("col") == 0) == (part == 0), 1, 0)


def halves(value):
    high = value.astype(jnp.bfloat16)
    return high, (value - high.astype(jnp.float32)).astype(jnp.bfloat16)


def times(stack, high, low):
    depth = stack.shape[0] // 2
    both = jnp.dot(stack[...], high, preferred_element_type=jnp.float32)
    rest = jnp.dot(stack[:depth], low, preferred_element_type=jnp.float32)
    return both[:depth] + (both[depth:] + rest)


def fetch_rows(starts, size, bounds, sources, stack, raw, sems):
    for index in range(starts.shape[-1]):
        start = looked_up(starts[..., index])
        first = 0
        for source, last in zip(sources, bounds):

            @pl.when((start >= first) & (start < last))
            def _(source=source, first=first, start=start, index=index):
                pltpu.make_async_copy(
                    source.at[pl.ds(pl.multiple_of(start - first, size), size)],
                    raw.at[pl.ds(index * size, size)],
                    sems.at[index],
                ).start()

            first = last
    for index in range(starts.shape[-1]):
        pltpu.make_async_copy(
            sources[0].at[pl.ds(0, size)], raw.at[pl.ds(index * size, size)], sems.at[index]
        ).wait()
    depth = raw.shape[0]
    stack[:depth], stack[depth:] = halves(raw[...])


def product_kernel(starts, size, bounds, parts, split, *refs):
    count = len(bounds)
    sources, refs = refs[:count], refs[count:]
    columns, refs = refs[: 1 if split else 2 * parts], refs[1 if split else 2 * parts :]
    if starts is None:
        (stack,) = sources
    else:
        *refs, stack, raw, sems = refs
        fetch_rows(starts, size, bounds, sources, stack, raw, sems)
    outs = refs[-parts - (2 if split else 0) :]
    for part in range(parts):
        width = outs[part].shape[1]
        tile = min(LANES, width)
        for at in range(0, width, tile):
            here = slice(at, at + tile)
            if split:
                first = pl.multiple_of(side(split - 1) * width + at, tile)
                high, low = halves(columns[0][:, pl.ds(first, tile)])
                outs[1][:, here], outs[2][:, here] = high, low
            else:
                high, low = (ref[:, here] for ref in columns[2 * part : 2 * part + 2])
            outs[part][:, here] = times(stack, high, low)


def product(sources, starts, size, columns, split, keep, *after):
    again = starts is None
    depth = sources[0].shape[0] // 2 if again else starts.shape[-1] * size
    inner, width = columns[0].shape
    parts = max(len(columns) // 2, 1)
    width = width // 2 if split else width
    anywhere, whole = pl.BlockSpec(memory_space=pl.ANY), pl.BlockSpec(memory_space=pltpu.VMEM)
    outs = [jax.ShapeDtypeStruct((depth, width), jnp.float32)] * parts
    outs += [jax.ShapeDtypeStruct((inner, width), jnp.bfloat16)] * (2 if split else 0)
    scratch = []
    if not again:
        scratch = [pltpu.VMEM((depth, inner), jnp.float32), pltpu.SemaphoreType.DMA((starts.shape[-1],))]
        if keep:
            outs += [jax.ShapeDtypeStruct((2 * depth, inner), jnp.bfloat16)]
        else:
            scratch.insert(0, pltpu.VMEM((2 * depth, inner), jnp.bfloat16))
    bounds = list(np.cumsum([s.shape[0] for s in sources]))
    return pl.pallas_call(
        functools.partial(product_kernel, starts, size, bounds, parts, split),
        out_shape=outs,
        in_specs=[whole if again else anywhere] * len(sources) + [whole] * len(columns) + [anywhere] * len(after),
        out_specs=[whole] * len(outs),
        scratch_shapes=scratch,
        compiler_params=pltpu.CompilerParams(vmem_limit_bytes=16 * MIB),
        cost_estimate=pl.CostEstimate(
            flops=6 * depth * inner * width * parts,
            bytes_accessed=4 * depth * inner + 4 * (inner + depth) * width * parts,
            transcendentals=0,
        ),
        name="product",
    )(*sources, *columns, *after)


def finish_kernel(*refs):
    out_ref = refs[-1]
    for part in range(2):
        above, below, own = refs[3 * part : 3 * part + 3]
        width = own.shape[1]
        columns = pl.ds(pl.multiple_of(side(part) * width, width), width)
        out_ref[:, columns] = (above[...] + below[...]) + own[...]


def finish(*values):
    depth, width = values[0].shape
    return pl.pallas_call(
        finish_kernel,
        out_shape=jax.ShapeDtypeStruct((depth, 2 * width), jnp.float32),
        in_specs=[pl.BlockSpec(memory_space=pltpu.VMEM)] * 6,
        out_specs=pl.BlockSpec(memory_space=pltpu.VMEM),
        compiler_params=pltpu.CompilerParams(vmem_limit_bytes=8 * MIB),
        name="finish",
    )(*values)


def plan(order, rows, cols, size, chunks):
    place = np.zeros(rows, np.int64)
    place[order] = np.arange(rows)
    each, half = rows // cols, rows // 2
    needs = np.zeros((rows, cols, rows), np.int64)
    for core in range(cols):
        ways = (-1, 1) if core == 0 else (1, -1)
        steps = [half] + [way * (half - step) for step in range(1, half) for way in ways] + [0]
        for row in range(rows):
            needs[row, core] = [order[(place[row] + step) % rows] for step in steps]
    spots = [(2 * sum(chunks[:chunk]) + at, count) for chunk, count in enumerate(chunks) for at in range(count)]
    taken = np.zeros((rows, cols, rows), np.int64)
    given = np.zeros((rows, cols, each), np.int64)
    for row in range(rows):
        for core in range(cols):
            sent = [block for block in needs[row, cols - 1 - core] if block // each == core]
            given[row, core] = [(block - core * each) * size for block in sent]
            arrived = 0
            for k, block in enumerate(needs[row, core]):
                if block // each == core:
                    taken[row, core, k] = spots[sent.index(block)][0] * size
                else:
                    taken[row, core, k] = sum(spots[arrived]) * size
                    arrived += 1
    return taken, given


def solution(mesh):
    rows, cols = mesh.shape["row"], mesh.shape["col"]
    order = ring_order(mesh)
    group = max(rows // CALLS, 1)
    half = rows // 2
    swap = [(core, cols - 1 - core) for core in range(cols)]
    ways = [
        [
            (order[i] * cols + core, order[(i + (way if core else -way)) % rows] * cols + core)
            for i in range(rows)
            for core in range(cols)
        ]
        for way in (1, -1)
    ]

    def shards(inductance, current_rates):
        size = inductance.shape[0] * cols // rows
        spare = int(group > 1)
        chunks = [group + spare] + [group] * (rows // cols // group - 2) + [group - spare]
        taken, given = plan(order, rows, cols, size, chunks)
        sources, pairs, calls, stacks, made = [], {}, {}, {}, []

        def fetch(first, last, room, *after):
            wanted = slice(sum(chunks[:first]), sum(chunks[:last]))
            for own in pick(inductance, given[..., wanted], size, chunks[first:last], room, *after):
                sources.extend([own, lax.ppermute(own, "col", swap)])

        def term(index, part):
            call, at = divmod(index, group)
            if (call, part) not in calls:
                parts = [part] if call < 3 else [0, 1]
                starts = taken[..., call * group : (call + 1) * group]
                firsts = np.cumsum([0] + [each.shape[0] for each in sources])
                have = sources[: int(np.searchsorted(firsts, starts.max(), "right"))]
                if call in stacks:
                    have, starts = [stacks[call]], None
                keep = call < 3 and call not in stacks
                split = 0 if part in pairs else 1 + part
                columns = [current_rates] if split else [half for each in parts for half in pairs[each]]
                got = product(have, starts, size, columns, split, keep, *made[-1:])
                if split:
                    pairs[part] = got[1:3]
                if keep:
                    stacks[call] = got[-1]
                calls.update({(call, each): value for each, value in zip(parts, got)})
                made.append(got[0])
            return calls[call, part][at * size : (at + 1) * size]

        fetch(0, 1, 52)
        fetch(1, len(chunks), 48, sources[0])

        sums = [[None, None], [None, None]]
        for step in range(half):
            for late in (1, 0):
                for way in range(2):
                    part = (way + late) % 2
                    if step == 0 and late:
                        continue
                    value = term(2 * step - 1 + way if step else 0, part)
                    if sums[way][part] is not None:
                        value = sums[way][part] + value
                    sums[way][part] = lax.ppermute(value, ("row", "col"), ways[way])
        return finish(*(each for part in range(2) for each in (sums[0][part], sums[1][part], term(rows - 1, part))))

    placed = (P(("groups", "col"), "row"), P("row", ("groups", "col")))
    return jax.shard_map(
        shards, mesh=mesh, in_specs=placed, out_specs=P("row", ("groups", "col")), check_vma=False
    )
```

```python
import functools

import jax
import jax.numpy as jnp
import numpy as np
from jax import lax
from jax.experimental import pallas as pl
from jax.experimental.pallas import tpu as pltpu
from jax.sharding import PartitionSpec as P

CALLS = 8
LANES = 256
PIECE = 16
MIB = 2**20


def ring_order(mesh):
    count = mesh.shape["row"]
    axes = list(mesh.axis_names)
    line = np.moveaxis(mesh.devices, axes.index("row"), 0).reshape(count, -1)[:, 0]
    spots = [tuple(device.coords) for device in line]
    moving = [axis for axis in range(3) if len({spot[axis] for spot in spots}) > 1]
    plain = list(range(count))
    if len(moving) != 2:
        return plain
    for outer, inner in (moving, moving[::-1]):
        across = sorted({spot[outer] for spot in spots})
        along = sorted({spot[inner] for spot in spots})
        if len(across) % 2 or len(across) * len(along) != count:
            continue
        at = {(spot[outer], spot[inner]): index for index, spot in enumerate(spots)}
        walk = [at[across[0], along[0]]]
        for turn, a in enumerate(across):
            rest = along[1:]
            walk += [at[a, b] for b in (rest if turn % 2 == 0 else rest[::-1])]
        walk += [at[a, along[0]] for a in across[:0:-1]]
        return walk
    return plain


def looked_up(table):
    row, col = lax.axis_index("row"), lax.axis_index("col")
    found = jnp.int32(0)
    for r in range(table.shape[0]):
        for c in range(table.shape[1]):
            found = jnp.where((row == r) & (col == c), jnp.int32(table[r, c]), found)
    return found


def pick_kernel(starts, size, chunks, a_ref, *refs):
    outs, sems = refs[-1 - len(chunks) : -1], refs[-1]
    spots = [(chunk, at * size) for chunk, count in enumerate(chunks) for at in range(count)]
    piece = min(size, PIECE)
    for index, (chunk, first) in enumerate(spots):
        start = looked_up(starts[..., index])
        for at in range(0, size, piece):
            pltpu.make_async_copy(
                a_ref.at[pl.ds(pl.multiple_of(start + at, piece), piece)],
                outs[chunk].at[pl.ds(first + at, piece)],
                sems.at[chunk],
            ).start()
    for chunk, out_ref in enumerate(outs):
        pltpu.make_async_copy(a_ref.at[pl.ds(0, out_ref.shape[0])], out_ref, sems.at[chunk]).wait()


def pick(inductance, starts, size, chunks, room, *after):
    width = inductance.shape[1]
    moved = 8 * sum(chunks) * size * width
    return pl.pallas_call(
        functools.partial(pick_kernel, starts, size, chunks),
        out_shape=[jax.ShapeDtypeStruct((count * size, width), jnp.float32) for count in chunks],
        in_specs=[pl.BlockSpec(memory_space=pl.ANY)] * (1 + len(after)),
        out_specs=[pl.BlockSpec(memory_space=pltpu.VMEM)] * len(chunks),
        scratch_shapes=[pltpu.SemaphoreType.DMA((len(chunks),))],
        compiler_params=pltpu.CompilerParams(vmem_limit_bytes=room * MIB),
        cost_estimate=pl.CostEstimate(flops=0, bytes_accessed=moved, transcendentals=0),
        name="pick",
    )(inductance, *after)


def side(part):
    return jnp.where((lax.axis_index("col") == 0) == (part == 0), 1, 0)


def halves(value):
    high = value.astype(jnp.bfloat16)
    return high, (value - high.astype(jnp.float32)).astype(jnp.bfloat16)


def times(stack, high, low):
    depth = stack.shape[0] // 2
    both = jnp.dot(stack[...], high, preferred_element_type=jnp.float32)
    rest = jnp.dot(stack[:depth], low, preferred_element_type=jnp.float32)
    return both[:depth] + (both[depth:] + rest)


def fetch_rows(starts, size, bounds, sources, stack, raw, sems):
    for index in range(starts.shape[-1]):
        start = looked_up(starts[..., index])
        first = 0
        for source, last in zip(sources, bounds):

            @pl.when((start >= first) & (start < last))
            def _(source=source, first=first, start=start, index=index):
                pltpu.make_async_copy(
                    source.at[pl.ds(pl.multiple_of(start - first, size), size)],
                    raw.at[pl.ds(index * size, size)],
                    sems.at[index],
                ).start()

            first = last
    for index in range(starts.shape[-1]):
        pltpu.make_async_copy(
            sources[0].at[pl.ds(0, size)], raw.at[pl.ds(index * size, size)], sems.at[index]
        ).wait()
    depth = raw.shape[0]
    stack[:depth], stack[depth:] = halves(raw[...])


def split_rows(starts, size, bounds, sources, stack):
    depth = stack.shape[0] // 2
    for index in range(starts.shape[-1]):
        start = looked_up(starts[..., index])
        at, first = index * size, 0
        for source, last in zip(sources, bounds):

            @pl.when((start >= first) & (start < last))
            def _(source=source, first=first, start=start, at=at):
                rows = source[...] if source.shape[0] == size else source[pl.ds(pl.multiple_of(start - first, size), size)]
                stack[at : at + size], stack[depth + at : depth + at + size] = halves(rows)

            first = last


def product_kernel(starts, size, bounds, parts, split, *refs):
    count = len(bounds)
    sources, refs = refs[:count], refs[count:]
    columns, refs = refs[: 1 if split else 2 * parts], refs[1 if split else 2 * parts :]
    if starts is None:
        (stack,) = sources
    else:
        *refs, stack, raw, sems = refs
        if split:
            split_rows(starts, size, bounds, sources, stack)
        else:
            fetch_rows(starts, size, bounds, sources, stack, raw, sems)
    outs = refs[-parts - (2 if split else 0) :]
    for part in range(parts):
        width = outs[part].shape[1]
        tile = min(LANES, width)
        for at in range(0, width, tile):
            here = slice(at, at + tile)
            if split:
                first = pl.multiple_of(side(split - 1) * width + at, tile)
                high, low = halves(columns[0][:, pl.ds(first, tile)])
                outs[1][:, here], outs[2][:, here] = high, low
            else:
                high, low = (ref[:, here] for ref in columns[2 * part : 2 * part + 2])
            outs[part][:, here] = times(stack, high, low)


def product(sources, starts, size, columns, split, keep, *after):
    again = starts is None
    depth = sources[0].shape[0] // 2 if again else starts.shape[-1] * size
    inner, width = columns[0].shape
    parts = max(len(columns) // 2, 1)
    width = width // 2 if split else width
    anywhere, whole = pl.BlockSpec(memory_space=pl.ANY), pl.BlockSpec(memory_space=pltpu.VMEM)
    outs = [jax.ShapeDtypeStruct((depth, width), jnp.float32)] * parts
    outs += [jax.ShapeDtypeStruct((inner, width), jnp.bfloat16)] * (2 if split else 0)
    scratch = []
    if not again:
        scratch = [pltpu.VMEM((depth, inner), jnp.float32), pltpu.SemaphoreType.DMA((starts.shape[-1],))]
        if keep:
            outs += [jax.ShapeDtypeStruct((2 * depth, inner), jnp.bfloat16)]
        else:
            scratch.insert(0, pltpu.VMEM((2 * depth, inner), jnp.bfloat16))
    bounds = list(np.cumsum([s.shape[0] for s in sources]))
    return pl.pallas_call(
        functools.partial(product_kernel, starts, size, bounds, parts, split),
        out_shape=outs,
        in_specs=[whole if again or split else anywhere] * len(sources) + [whole] * len(columns) + [anywhere] * len(after),
        out_specs=[whole] * len(outs),
        scratch_shapes=scratch,
        compiler_params=pltpu.CompilerParams(vmem_limit_bytes=16 * MIB),
        cost_estimate=pl.CostEstimate(
            flops=6 * depth * inner * width * parts,
            bytes_accessed=4 * depth * inner + 4 * (inner + depth) * width * parts,
            transcendentals=0,
        ),
        name="product",
    )(*sources, *columns, *after)


def finish_kernel(*refs):
    out_ref = refs[-1]
    for part in range(2):
        above, below, own = refs[3 * part : 3 * part + 3]
        width = own.shape[1]
        columns = pl.ds(pl.multiple_of(side(part) * width, width), width)
        out_ref[:, columns] = (above[...] + below[...]) + own[...]


def finish(*values):
    depth, width = values[0].shape
    return pl.pallas_call(
        finish_kernel,
        out_shape=jax.ShapeDtypeStruct((depth, 2 * width), jnp.float32),
        in_specs=[pl.BlockSpec(memory_space=pltpu.VMEM)] * 6,
        out_specs=pl.BlockSpec(memory_space=pltpu.VMEM),
        compiler_params=pltpu.CompilerParams(vmem_limit_bytes=8 * MIB),
        name="finish",
    )(*values)


def plan(order, rows, cols, size, chunks):
    place = np.zeros(rows, np.int64)
    place[order] = np.arange(rows)
    each, half = rows // cols, rows // 2
    needs = np.zeros((rows, cols, rows), np.int64)
    for core in range(cols):
        ways = (-1, 1) if core == 0 else (1, -1)
        steps = [half] + [way * (half - step) for step in range(1, half) for way in ways] + [0]
        for row in range(rows):
            needs[row, core] = [order[(place[row] + step) % rows] for step in steps]
    spots = [(2 * sum(chunks[:chunk]) + at, count) for chunk, count in enumerate(chunks) for at in range(count)]
    taken = np.zeros((rows, cols, rows), np.int64)
    given = np.zeros((rows, cols, each), np.int64)
    for row in range(rows):
        for core in range(cols):
            sent = [block for block in needs[row, cols - 1 - core] if block // each == core]
            given[row, core] = [(block - core * each) * size for block in sent]
            arrived = 0
            for k, block in enumerate(needs[row, core]):
                if block // each == core:
                    taken[row, core, k] = spots[sent.index(block)][0] * size
                else:
                    taken[row, core, k] = sum(spots[arrived]) * size
                    arrived += 1
    return taken, given


def solution(mesh):
    rows, cols = mesh.shape["row"], mesh.shape["col"]
    order = ring_order(mesh)
    group = max(rows // CALLS, 1)
    half = rows // 2
    swap = [(core, cols - 1 - core) for core in range(cols)]
    ways = [
        [
            (order[i] * cols + core, order[(i + (way if core else -way)) % rows] * cols + core)
            for i in range(rows)
            for core in range(cols)
        ]
        for way in (1, -1)
    ]

    def shards(inductance, current_rates):
        size = inductance.shape[0] * cols // rows
        spare = int(group > 1)
        chunks = [group + spare] + [group] * (rows // cols // group - 2) + [group - spare]
        taken, given = plan(order, rows, cols, size, chunks)
        sources, pairs, calls, stacks, made = [], {}, {}, {}, []

        def fetch(first, last, room, *after):
            wanted = slice(sum(chunks[:first]), sum(chunks[:last]))
            for own in pick(inductance, given[..., wanted], size, chunks[first:last], room, *after):
                sources.extend([own, lax.ppermute(own, "col", swap)])

        def term(index, part):
            call, at = divmod(index, group)
            if (call, part) not in calls:
                parts = [part] if call < 3 else [0, 1]
                starts = taken[..., call * group : (call + 1) * group]
                firsts = np.cumsum([0] + [each.shape[0] for each in sources])
                have = sources[: int(np.searchsorted(firsts, starts.max(), "right"))]
                if call in stacks:
                    have, starts = [stacks[call]], None
                keep = call < 3 and call not in stacks
                split = 0 if part in pairs else 1 + part
                columns = [current_rates] if split else [half for each in parts for half in pairs[each]]
                got = product(have, starts, size, columns, split, keep, *made[-1:])
                if split:
                    pairs[part] = got[1:3]
                if keep:
                    stacks[call] = got[-1]
                calls.update({(call, each): value for each, value in zip(parts, got)})
                made.append(got[0])
            return calls[call, part][at * size : (at + 1) * size]

        fetch(0, 1, 52)
        fetch(1, len(chunks), 48, sources[0])

        sums = [[None, None], [None, None]]
        for step in range(half):
            for late in (1, 0):
                for way in range(2):
                    part = (way + late) % 2
                    if step == 0 and late:
                        continue
                    value = term(2 * step - 1 + way if step else 0, part)
                    if sums[way][part] is not None:
                        value = sums[way][part] + value
                    sums[way][part] = lax.ppermute(value, ("row", "col"), ways[way])
        return finish(*(each for part in range(2) for each in (sums[0][part], sums[1][part], term(rows - 1, part))))

    placed = (P(("groups", "col"), "row"), P("row", ("groups", "col")))
    return jax.shard_map(
        shards, mesh=mesh, in_specs=placed, out_specs=P("row", ("groups", "col")), check_vma=False
    )
```

```python
import functools

import jax
import jax.numpy as jnp
import numpy as np
from jax import lax
from jax.experimental import pallas as pl
from jax.experimental.pallas import tpu as pltpu
from jax.sharding import PartitionSpec as P

CALLS = 8
LANES = 256
PIECE = 16
MIB = 2**20


def ring_order(mesh):
    count = mesh.shape["row"]
    axes = list(mesh.axis_names)
    line = np.moveaxis(mesh.devices, axes.index("row"), 0).reshape(count, -1)[:, 0]
    spots = [tuple(device.coords) for device in line]
    moving = [axis for axis in range(3) if len({spot[axis] for spot in spots}) > 1]
    plain = list(range(count))
    if len(moving) != 2:
        return plain
    for outer, inner in (moving, moving[::-1]):
        across = sorted({spot[outer] for spot in spots})
        along = sorted({spot[inner] for spot in spots})
        if len(across) % 2 or len(across) * len(along) != count:
            continue
        at = {(spot[outer], spot[inner]): index for index, spot in enumerate(spots)}
        walk = [at[across[0], along[0]]]
        for turn, a in enumerate(across):
            rest = along[1:]
            walk += [at[a, b] for b in (rest if turn % 2 == 0 else rest[::-1])]
        walk += [at[a, along[0]] for a in across[:0:-1]]
        return walk
    return plain


def looked_up(table):
    row, col = lax.axis_index("row"), lax.axis_index("col")
    found = jnp.int32(0)
    for r in range(table.shape[0]):
        for c in range(table.shape[1]):
            found = jnp.where((row == r) & (col == c), jnp.int32(table[r, c]), found)
    return found


def pick_kernel(starts, size, chunks, a_ref, *refs):
    outs, sems = refs[-1 - len(chunks) : -1], refs[-1]
    spots = [(chunk, at * size) for chunk, count in enumerate(chunks) for at in range(count)]
    piece = min(size, PIECE)
    for index, (chunk, first) in enumerate(spots):
        start = looked_up(starts[..., index])
        for at in range(0, size, piece):
            pltpu.make_async_copy(
                a_ref.at[pl.ds(pl.multiple_of(start + at, piece), piece)],
                outs[chunk].at[pl.ds(first + at, piece)],
                sems.at[chunk],
            ).start()
    for chunk, out_ref in enumerate(outs):
        pltpu.make_async_copy(a_ref.at[pl.ds(0, out_ref.shape[0])], out_ref, sems.at[chunk]).wait()


def pick(inductance, starts, size, chunks, room, *after):
    width = inductance.shape[1]
    moved = 8 * sum(chunks) * size * width
    return pl.pallas_call(
        functools.partial(pick_kernel, starts, size, chunks),
        out_shape=[jax.ShapeDtypeStruct((count * size, width), jnp.float32) for count in chunks],
        in_specs=[pl.BlockSpec(memory_space=pl.ANY)] * (1 + len(after)),
        out_specs=[pl.BlockSpec(memory_space=pltpu.VMEM)] * len(chunks),
        scratch_shapes=[pltpu.SemaphoreType.DMA((len(chunks),))],
        compiler_params=pltpu.CompilerParams(vmem_limit_bytes=room * MIB),
        cost_estimate=pl.CostEstimate(flops=0, bytes_accessed=moved, transcendentals=0),
        name="pick",
    )(inductance, *after)


def side(part):
    return jnp.where((lax.axis_index("col") == 0) == (part == 0), 1, 0)


def halves(value):
    high = value.astype(jnp.bfloat16)
    return high, (value - high.astype(jnp.float32)).astype(jnp.bfloat16)


def times(stack, high, low):
    depth = stack.shape[0] // 2
    both = jnp.dot(stack[...], high, preferred_element_type=jnp.float32)
    rest = jnp.dot(stack[:depth], low, preferred_element_type=jnp.float32)
    return both[:depth] + (both[depth:] + rest)


def fetch_rows(starts, size, bounds, sources, stack, raw, sems):
    for index in range(starts.shape[-1]):
        start = looked_up(starts[..., index])
        first = 0
        for source, last in zip(sources, bounds):

            @pl.when((start >= first) & (start < last))
            def _(source=source, first=first, start=start, index=index):
                pltpu.make_async_copy(
                    source.at[pl.ds(pl.multiple_of(start - first, size), size)],
                    raw.at[pl.ds(index * size, size)],
                    sems.at[index],
                ).start()

            first = last
    for index in range(starts.shape[-1]):
        pltpu.make_async_copy(
            sources[0].at[pl.ds(0, size)], raw.at[pl.ds(index * size, size)], sems.at[index]
        ).wait()
    depth = raw.shape[0]
    stack[:depth], stack[depth:] = halves(raw[...])


def split_rows(starts, size, bounds, sources, stack):
    depth = stack.shape[0] // 2
    for index in range(starts.shape[-1]):
        start = looked_up(starts[..., index])
        at, first = index * size, 0
        for source, last in zip(sources, bounds):

            @pl.when((start >= first) & (start < last))
            def _(source=source, first=first, start=start, at=at):
                rows = source[...] if source.shape[0] == size else source[pl.ds(pl.multiple_of(start - first, size), size)]
                stack[at : at + size], stack[depth + at : depth + at + size] = halves(rows)

            first = last


def product_kernel(starts, size, bounds, parts, split, *refs):
    count = len(bounds)
    sources, refs = refs[:count], refs[count:]
    columns, refs = refs[: 1 if split else 2 * parts], refs[1 if split else 2 * parts :]
    if starts is None:
        (stack,) = sources
    else:
        *refs, stack, raw, sems = refs
        if split:
            split_rows(starts, size, bounds, sources, stack)
        else:
            fetch_rows(starts, size, bounds, sources, stack, raw, sems)
    outs = refs[-parts - (2 if split else 0) :]
    for part in range(parts):
        width = outs[part].shape[1]
        tile = min(LANES, width)
        for at in range(0, width, tile):
            here = slice(at, at + tile)
            if split:
                first = pl.multiple_of(side(split - 1) * width + at, tile)
                high, low = halves(columns[0][:, pl.ds(first, tile)])
                outs[1][:, here], outs[2][:, here] = high, low
            else:
                high, low = (ref[:, here] for ref in columns[2 * part : 2 * part + 2])
            outs[part][:, here] = times(stack, high, low)


def product(sources, starts, size, columns, split, keep, *after):
    again = starts is None
    depth = sources[0].shape[0] // 2 if again else starts.shape[-1] * size
    inner, width = columns[0].shape
    parts = max(len(columns) // 2, 1)
    width = width // 2 if split else width
    anywhere, whole = pl.BlockSpec(memory_space=pl.ANY), pl.BlockSpec(memory_space=pltpu.VMEM)
    outs = [jax.ShapeDtypeStruct((depth, width), jnp.float32)] * parts
    outs += [jax.ShapeDtypeStruct((inner, width), jnp.bfloat16)] * (2 if split else 0)
    scratch = []
    if not again:
        scratch = [pltpu.VMEM((depth, inner), jnp.float32), pltpu.SemaphoreType.DMA((starts.shape[-1],))]
        if keep:
            outs += [jax.ShapeDtypeStruct((2 * depth, inner), jnp.bfloat16)]
        else:
            scratch.insert(0, pltpu.VMEM((2 * depth, inner), jnp.bfloat16))
    bounds = list(np.cumsum([s.shape[0] for s in sources]))
    return pl.pallas_call(
        functools.partial(product_kernel, starts, size, bounds, parts, split),
        out_shape=outs,
        in_specs=[whole if again or split else anywhere] * len(sources) + [whole] * len(columns) + [anywhere] * len(after),
        out_specs=[whole] * len(outs),
        scratch_shapes=scratch,
        compiler_params=pltpu.CompilerParams(vmem_limit_bytes=16 * MIB),
        cost_estimate=pl.CostEstimate(
            flops=6 * depth * inner * width * parts,
            bytes_accessed=4 * depth * inner + 4 * (inner + depth) * width * parts,
            transcendentals=0,
        ),
        name="product",
    )(*sources, *columns, *after)


def finish_kernel(*refs):
    out_ref = refs[-1]
    for part in range(2):
        above, below, own = refs[3 * part : 3 * part + 3]
        width = own.shape[1]
        columns = pl.ds(pl.multiple_of(side(part) * width, width), width)
        out_ref[:, columns] = (above[...] + below[...]) + own[...]


def finish(*values):
    depth, width = values[0].shape
    return pl.pallas_call(
        finish_kernel,
        out_shape=jax.ShapeDtypeStruct((depth, 2 * width), jnp.float32),
        in_specs=[pl.BlockSpec(memory_space=pltpu.VMEM)] * 6,
        out_specs=pl.BlockSpec(memory_space=pltpu.VMEM),
        compiler_params=pltpu.CompilerParams(vmem_limit_bytes=8 * MIB),
        name="finish",
    )(*values)


def plan(order, rows, cols, size, chunks):
    place = np.zeros(rows, np.int64)
    place[order] = np.arange(rows)
    each, half = rows // cols, rows // 2
    needs = np.zeros((rows, cols, rows), np.int64)
    for core in range(cols):
        ways = (-1, 1) if core == 0 else (1, -1)
        steps = [half] + [way * (half - step) for step in range(1, half) for way in ways] + [0]
        for row in range(rows):
            needs[row, core] = [order[(place[row] + step) % rows] for step in steps]
    spots = [(2 * sum(chunks[:chunk]) + at, count) for chunk, count in enumerate(chunks) for at in range(count)]
    taken = np.zeros((rows, cols, rows), np.int64)
    given = np.zeros((rows, cols, each), np.int64)
    for row in range(rows):
        for core in range(cols):
            sent = [block for block in needs[row, cols - 1 - core] if block // each == core]
            given[row, core] = [(block - core * each) * size for block in sent]
            arrived = 0
            for k, block in enumerate(needs[row, core]):
                if block // each == core:
                    taken[row, core, k] = spots[sent.index(block)][0] * size
                else:
                    taken[row, core, k] = sum(spots[arrived]) * size
                    arrived += 1
    return taken, given


def solution(mesh):
    rows, cols = mesh.shape["row"], mesh.shape["col"]
    order = ring_order(mesh)
    group = max(rows // CALLS, 1)
    half = rows // 2
    swap = [(core, cols - 1 - core) for core in range(cols)]
    ways = [
        [
            (order[i] * cols + core, order[(i + (way if core else -way)) % rows] * cols + core)
            for i in range(rows)
            for core in range(cols)
        ]
        for way in (1, -1)
    ]

    def shards(inductance, current_rates):
        size = inductance.shape[0] * cols // rows
        spare = int(group > 1)
        chunks = [group + spare] + [group] * (rows // cols // group - 2) + [group - spare]
        taken, given = plan(order, rows, cols, size, chunks)
        sources, pairs, calls, stacks, made = [], {}, {}, {}, []

        def fetch(first, last, room, *after):
            wanted = slice(sum(chunks[:first]), sum(chunks[:last]))
            for own in pick(inductance, given[..., wanted], size, chunks[first:last], room, *after):
                sources.extend([own, lax.ppermute(own, "col", swap)])

        def term(index, part):
            call, at = divmod(index, group)
            if (call, part) not in calls:
                parts = [part] if call < 3 else [0, 1]
                starts = taken[..., call * group : (call + 1) * group]
                firsts = np.cumsum([0] + [each.shape[0] for each in sources])
                have = sources[: int(np.searchsorted(firsts, starts.max(), "right"))]
                if call in stacks:
                    have, starts = [stacks[call]], None
                keep = call < 3 and call not in stacks
                split = 0 if part in pairs else 1 + part
                columns = [current_rates] if split else [half for each in parts for half in pairs[each]]
                got = product(have, starts, size, columns, split, keep, *made[-1:])
                if split:
                    pairs[part] = got[1:3]
                if keep:
                    stacks[call] = got[-1]
                calls.update({(call, each): value for each, value in zip(parts, got)})
                made.append(got[0])
            return calls[call, part][at * size : (at + 1) * size]

        fetch(0, 2, 50)
        fetch(2, len(chunks), 48, sources[0])

        sums = [[None, None], [None, None]]
        for step in range(half):
            for late in (1, 0):
                for way in range(2):
                    part = (way + late) % 2
                    if step == 0 and late:
                        continue
                    value = term(2 * step - 1 + way if step else 0, part)
                    if sums[way][part] is not None:
                        value = sums[way][part] + value
                    sums[way][part] = lax.ppermute(value, ("row", "col"), ways[way])
        return finish(*(each for part in range(2) for each in (sums[0][part], sums[1][part], term(rows - 1, part))))

    placed = (P(("groups", "col"), "row"), P("row", ("groups", "col")))
    return jax.shard_map(
        shards, mesh=mesh, in_specs=placed, out_specs=P("row", ("groups", "col")), check_vma=False
    )
```

```python
import functools

import jax
import jax.numpy as jnp
import numpy as np
from jax import lax
from jax.experimental import pallas as pl
from jax.experimental.pallas import tpu as pltpu
from jax.sharding import PartitionSpec as P

CALLS = 8
LANES = 256
SLAB = 512
PIECE = 16
MIB = 2**20


def ring_order(mesh):
    count = mesh.shape["row"]
    axes = list(mesh.axis_names)
    line = np.moveaxis(mesh.devices, axes.index("row"), 0).reshape(count, -1)[:, 0]
    spots = [tuple(device.coords) for device in line]
    moving = [axis for axis in range(3) if len({spot[axis] for spot in spots}) > 1]
    plain = list(range(count))
    if len(moving) != 2:
        return plain
    for outer, inner in (moving, moving[::-1]):
        across = sorted({spot[outer] for spot in spots})
        along = sorted({spot[inner] for spot in spots})
        if len(across) % 2 or len(across) * len(along) != count:
            continue
        at = {(spot[outer], spot[inner]): index for index, spot in enumerate(spots)}
        walk = [at[across[0], along[0]]]
        for turn, a in enumerate(across):
            rest = along[1:]
            walk += [at[a, b] for b in (rest if turn % 2 == 0 else rest[::-1])]
        walk += [at[a, along[0]] for a in across[:0:-1]]
        return walk
    return plain


def looked_up(table):
    row, col = lax.axis_index("row"), lax.axis_index("col")
    found = jnp.int32(0)
    for r in range(table.shape[0]):
        for c in range(table.shape[1]):
            found = jnp.where((row == r) & (col == c), jnp.int32(table[r, c]), found)
    return found


def pick_kernel(starts, size, chunks, a_ref, *refs):
    outs, sems = refs[-1 - len(chunks) : -1], refs[-1]
    spots = [(chunk, at * size) for chunk, count in enumerate(chunks) for at in range(count)]
    piece = min(size, PIECE)
    for index, (chunk, first) in enumerate(spots):
        start = looked_up(starts[..., index])
        for at in range(0, size, piece):
            pltpu.make_async_copy(
                a_ref.at[pl.ds(pl.multiple_of(start + at, piece), piece)],
                outs[chunk].at[pl.ds(first + at, piece)],
                sems.at[chunk],
            ).start()
    for chunk, out_ref in enumerate(outs):
        pltpu.make_async_copy(a_ref.at[pl.ds(0, out_ref.shape[0])], out_ref, sems.at[chunk]).wait()


def pick(inductance, starts, size, chunks, room, *after):
    width = inductance.shape[1]
    moved = 8 * sum(chunks) * size * width
    return pl.pallas_call(
        functools.partial(pick_kernel, starts, size, chunks),
        out_shape=[jax.ShapeDtypeStruct((count * size, width), jnp.float32) for count in chunks],
        in_specs=[pl.BlockSpec(memory_space=pl.ANY)] * (1 + len(after)),
        out_specs=[pl.BlockSpec(memory_space=pltpu.VMEM)] * len(chunks),
        scratch_shapes=[pltpu.SemaphoreType.DMA((len(chunks),))],
        compiler_params=pltpu.CompilerParams(vmem_limit_bytes=room * MIB),
        cost_estimate=pl.CostEstimate(flops=0, bytes_accessed=moved, transcendentals=0),
        name="pick",
    )(inductance, *after)


def side(part):
    return jnp.where((lax.axis_index("col") == 0) == (part == 0), 1, 0)


def halves(value):
    high = value.astype(jnp.bfloat16)
    return high, (value - high.astype(jnp.float32)).astype(jnp.bfloat16)


def times(stack, high, low):
    depth = stack.shape[0] // 2
    both = jnp.dot(stack, high, preferred_element_type=jnp.float32)
    rest = jnp.dot(stack[:depth], low, preferred_element_type=jnp.float32)
    return both[:depth] + (both[depth:] + rest)


def fetch_rows(starts, size, bounds, sources, stack, raw, sems):
    for index in range(starts.shape[-1]):
        start = looked_up(starts[..., index])
        first = 0
        for source, last in zip(sources, bounds):

            @pl.when((start >= first) & (start < last))
            def _(source=source, first=first, start=start, index=index):
                pltpu.make_async_copy(
                    source.at[pl.ds(pl.multiple_of(start - first, size), size)],
                    raw.at[pl.ds(index * size, size)],
                    sems.at[index],
                ).start()

            first = last
    for index in range(starts.shape[-1]):
        pltpu.make_async_copy(
            sources[0].at[pl.ds(0, size)], raw.at[pl.ds(index * size, size)], sems.at[index]
        ).wait()
    depth = raw.shape[0]
    stack[:depth], stack[depth:] = halves(raw[...])


def split_rows(starts, size, bounds, sources, stack):
    depth = stack.shape[0] // 2
    for index in range(starts.shape[-1]):
        start = looked_up(starts[..., index])
        at, first = index * size, 0
        for source, last in zip(sources, bounds):

            @pl.when((start >= first) & (start < last))
            def _(source=source, first=first, start=start, at=at):
                rows = source[...] if source.shape[0] == size else source[pl.ds(pl.multiple_of(start - first, size), size)]
                stack[at : at + size], stack[depth + at : depth + at + size] = halves(rows)

            first = last


def product_kernel(starts, size, bounds, parts, split, *refs):
    count = len(bounds)
    sources, refs = refs[:count], refs[count:]
    columns, refs = refs[: 1 if split else 2 * parts], refs[1 if split else 2 * parts :]
    if starts is None:
        (stack,) = sources
    else:
        *refs, stack, raw, sems = refs
        if split:
            split_rows(starts, size, bounds, sources, stack)
        else:
            fetch_rows(starts, size, bounds, sources, stack, raw, sems)
    outs = refs[-parts - (2 if split else 0) :]
    for part in range(parts):
        width = outs[part].shape[1]
        tile = min(LANES, width)
        for at in range(0, width, tile):
            here = slice(at, at + tile)
            if split:
                first = pl.multiple_of(side(split - 1) * width + at, tile)
                depth, inner = stack.shape[0] // 2, stack.shape[1]
                slab = min(SLAB, inner)
                total = jnp.zeros((depth, tile), jnp.float32)
                for top in range(0, inner, slab):
                    deep = slice(top, top + slab)
                    high, low = halves(columns[0][deep, pl.ds(first, tile)])
                    outs[1][deep, here], outs[2][deep, here] = high, low
                    total += times(stack[:, deep], high, low)
                outs[part][:, here] = total
            else:
                high, low = (ref[:, here] for ref in columns[2 * part : 2 * part + 2])
                outs[part][:, here] = times(stack[...], high, low)


def product(sources, starts, size, columns, split, keep, *after):
    again = starts is None
    depth = sources[0].shape[0] // 2 if again else starts.shape[-1] * size
    inner, width = columns[0].shape
    parts = max(len(columns) // 2, 1)
    width = width // 2 if split else width
    anywhere, whole = pl.BlockSpec(memory_space=pl.ANY), pl.BlockSpec(memory_space=pltpu.VMEM)
    outs = [jax.ShapeDtypeStruct((depth, width), jnp.float32)] * parts
    outs += [jax.ShapeDtypeStruct((inner, width), jnp.bfloat16)] * (2 if split else 0)
    scratch = []
    if not again:
        scratch = [pltpu.VMEM((depth, inner), jnp.float32), pltpu.SemaphoreType.DMA((starts.shape[-1],))]
        if keep:
            outs += [jax.ShapeDtypeStruct((2 * depth, inner), jnp.bfloat16)]
        else:
            scratch.insert(0, pltpu.VMEM((2 * depth, inner), jnp.bfloat16))
    bounds = list(np.cumsum([s.shape[0] for s in sources]))
    return pl.pallas_call(
        functools.partial(product_kernel, starts, size, bounds, parts, split),
        out_shape=outs,
        in_specs=[whole if again or split else anywhere] * len(sources) + [whole] * len(columns) + [anywhere] * len(after),
        out_specs=[whole] * len(outs),
        scratch_shapes=scratch,
        compiler_params=pltpu.CompilerParams(vmem_limit_bytes=16 * MIB),
        cost_estimate=pl.CostEstimate(
            flops=6 * depth * inner * width * parts,
            bytes_accessed=4 * depth * inner + 4 * (inner + depth) * width * parts,
            transcendentals=0,
        ),
        name="product",
    )(*sources, *columns, *after)


def finish_kernel(*refs):
    out_ref = refs[-1]
    for part in range(2):
        above, below, own = refs[3 * part : 3 * part + 3]
        width = own.shape[1]
        columns = pl.ds(pl.multiple_of(side(part) * width, width), width)
        out_ref[:, columns] = (above[...] + below[...]) + own[...]


def finish(*values):
    depth, width = values[0].shape
    return pl.pallas_call(
        finish_kernel,
        out_shape=jax.ShapeDtypeStruct((depth, 2 * width), jnp.float32),
        in_specs=[pl.BlockSpec(memory_space=pltpu.VMEM)] * 6,
        out_specs=pl.BlockSpec(memory_space=pltpu.VMEM),
        compiler_params=pltpu.CompilerParams(vmem_limit_bytes=8 * MIB),
        name="finish",
    )(*values)


def plan(order, rows, cols, size, chunks):
    place = np.zeros(rows, np.int64)
    place[order] = np.arange(rows)
    each, half = rows // cols, rows // 2
    needs = np.zeros((rows, cols, rows), np.int64)
    for core in range(cols):
        ways = (-1, 1) if core == 0 else (1, -1)
        steps = [half] + [way * (half - step) for step in range(1, half) for way in ways] + [0]
        for row in range(rows):
            needs[row, core] = [order[(place[row] + step) % rows] for step in steps]
    spots = [(2 * sum(chunks[:chunk]) + at, count) for chunk, count in enumerate(chunks) for at in range(count)]
    taken = np.zeros((rows, cols, rows), np.int64)
    given = np.zeros((rows, cols, each), np.int64)
    for row in range(rows):
        for core in range(cols):
            sent = [block for block in needs[row, cols - 1 - core] if block // each == core]
            given[row, core] = [(block - core * each) * size for block in sent]
            arrived = 0
            for k, block in enumerate(needs[row, core]):
                if block // each == core:
                    taken[row, core, k] = spots[sent.index(block)][0] * size
                else:
                    taken[row, core, k] = sum(spots[arrived]) * size
                    arrived += 1
    return taken, given


def solution(mesh):
    rows, cols = mesh.shape["row"], mesh.shape["col"]
    order = ring_order(mesh)
    group = max(rows // CALLS, 1)
    half = rows // 2
    swap = [(core, cols - 1 - core) for core in range(cols)]
    ways = [
        [
            (order[i] * cols + core, order[(i + (way if core else -way)) % rows] * cols + core)
            for i in range(rows)
            for core in range(cols)
        ]
        for way in (1, -1)
    ]

    def shards(inductance, current_rates):
        size = inductance.shape[0] * cols // rows
        spare = int(group > 1)
        chunks = [group + spare] + [group] * (rows // cols // group - 2) + [group - spare]
        taken, given = plan(order, rows, cols, size, chunks)
        sources, pairs, calls, stacks, made = [], {}, {}, {}, []

        def fetch(first, last, room, *after):
            wanted = slice(sum(chunks[:first]), sum(chunks[:last]))
            for own in pick(inductance, given[..., wanted], size, chunks[first:last], room, *after):
                sources.extend([own, lax.ppermute(own, "col", swap)])

        def term(index, part):
            call, at = divmod(index, group)
            if (call, part) not in calls:
                parts = [part] if call < 3 else [0, 1]
                starts = taken[..., call * group : (call + 1) * group]
                firsts = np.cumsum([0] + [each.shape[0] for each in sources])
                have = sources[: int(np.searchsorted(firsts, starts.max(), "right"))]
                if call in stacks:
                    have, starts = [stacks[call]], None
                keep = call < 3 and call not in stacks
                split = 0 if part in pairs else 1 + part
                columns = [current_rates] if split else [half for each in parts for half in pairs[each]]
                got = product(have, starts, size, columns, split, keep, *made[-1:])
                if split:
                    pairs[part] = got[1:3]
                if keep:
                    stacks[call] = got[-1]
                calls.update({(call, each): value for each, value in zip(parts, got)})
                made.append(got[0])
            return calls[call, part][at * size : (at + 1) * size]

        fetch(0, 1, 52)
        fetch(1, len(chunks), 48, sources[0])

        sums = [[None, None], [None, None]]
        for step in range(half):
            for late in (1, 0):
                for way in range(2):
                    part = (way + late) % 2
                    if step == 0 and late:
                        continue
                    value = term(2 * step - 1 + way if step else 0, part)
                    if sums[way][part] is not None:
                        value = sums[way][part] + value
                    sums[way][part] = lax.ppermute(value, ("row", "col"), ways[way])
        return finish(*(each for part in range(2) for each in (sums[0][part], sums[1][part], term(rows - 1, part))))

    placed = (P(("groups", "col"), "row"), P("row", ("groups", "col")))
    return jax.shard_map(
        shards, mesh=mesh, in_specs=placed, out_specs=P("row", ("groups", "col")), check_vma=False
    )
```

```python
import functools

import jax
import jax.numpy as jnp
import numpy as np
from jax import lax
from jax.experimental import pallas as pl
from jax.experimental.pallas import tpu as pltpu
from jax.sharding import PartitionSpec as P

CALLS = 8
LANES = 512
PIECE = 16
MIB = 2**20


def ring_order(mesh):
    count = mesh.shape["row"]
    axes = list(mesh.axis_names)
    line = np.moveaxis(mesh.devices, axes.index("row"), 0).reshape(count, -1)[:, 0]
    spots = [tuple(device.coords) for device in line]
    moving = [axis for axis in range(3) if len({spot[axis] for spot in spots}) > 1]
    plain = list(range(count))
    if len(moving) != 2:
        return plain
    for outer, inner in (moving, moving[::-1]):
        across = sorted({spot[outer] for spot in spots})
        along = sorted({spot[inner] for spot in spots})
        if len(across) % 2 or len(across) * len(along) != count:
            continue
        at = {(spot[outer], spot[inner]): index for index, spot in enumerate(spots)}
        walk = [at[across[0], along[0]]]
        for turn, a in enumerate(across):
            rest = along[1:]
            walk += [at[a, b] for b in (rest if turn % 2 == 0 else rest[::-1])]
        walk += [at[a, along[0]] for a in across[:0:-1]]
        return walk
    return plain


def looked_up(table):
    row, col = lax.axis_index("row"), lax.axis_index("col")
    found = jnp.int32(0)
    for r in range(table.shape[0]):
        for c in range(table.shape[1]):
            found = jnp.where((row == r) & (col == c), jnp.int32(table[r, c]), found)
    return found


def pick_kernel(starts, size, chunks, a_ref, *refs):
    outs, sems = refs[-1 - len(chunks) : -1], refs[-1]
    spots = [(chunk, at * size) for chunk, count in enumerate(chunks) for at in range(count)]
    piece = min(size, PIECE)
    for index, (chunk, first) in enumerate(spots):
        start = looked_up(starts[..., index])
        for at in range(0, size, piece):
            pltpu.make_async_copy(
                a_ref.at[pl.ds(pl.multiple_of(start + at, piece), piece)],
                outs[chunk].at[pl.ds(first + at, piece)],
                sems.at[chunk],
            ).start()
    for chunk, out_ref in enumerate(outs):
        pltpu.make_async_copy(a_ref.at[pl.ds(0, out_ref.shape[0])], out_ref, sems.at[chunk]).wait()


def pick(inductance, starts, size, chunks, room, *after):
    width = inductance.shape[1]
    moved = 8 * sum(chunks) * size * width
    return pl.pallas_call(
        functools.partial(pick_kernel, starts, size, chunks),
        out_shape=[jax.ShapeDtypeStruct((count * size, width), jnp.float32) for count in chunks],
        in_specs=[pl.BlockSpec(memory_space=pl.ANY)] * (1 + len(after)),
        out_specs=[pl.BlockSpec(memory_space=pltpu.VMEM)] * len(chunks),
        scratch_shapes=[pltpu.SemaphoreType.DMA((len(chunks),))],
        compiler_params=pltpu.CompilerParams(vmem_limit_bytes=room * MIB),
        cost_estimate=pl.CostEstimate(flops=0, bytes_accessed=moved, transcendentals=0),
        name="pick",
    )(inductance, *after)


def side(part):
    return jnp.where((lax.axis_index("col") == 0) == (part == 0), 1, 0)


def halves(value):
    high = value.astype(jnp.bfloat16)
    return high, (value - high.astype(jnp.float32)).astype(jnp.bfloat16)


def times(stack, high, low):
    depth = stack.shape[0] // 2
    both = jnp.dot(stack[...], high, preferred_element_type=jnp.float32)
    rest = jnp.dot(stack[:depth], low, preferred_element_type=jnp.float32)
    return both[:depth] + (both[depth:] + rest)


def fetch_rows(starts, size, bounds, sources, stack, raw, sems):
    for index in range(starts.shape[-1]):
        start = looked_up(starts[..., index])
        first = 0
        for source, last in zip(sources, bounds):

            @pl.when((start >= first) & (start < last))
            def _(source=source, first=first, start=start, index=index):
                pltpu.make_async_copy(
                    source.at[pl.ds(pl.multiple_of(start - first, size), size)],
                    raw.at[pl.ds(index * size, size)],
                    sems.at[index],
                ).start()

            first = last
    for index in range(starts.shape[-1]):
        pltpu.make_async_copy(
            sources[0].at[pl.ds(0, size)], raw.at[pl.ds(index * size, size)], sems.at[index]
        ).wait()
    depth = raw.shape[0]
    stack[:depth], stack[depth:] = halves(raw[...])


def split_rows(starts, size, bounds, sources, stack):
    depth = stack.shape[0] // 2
    for index in range(starts.shape[-1]):
        start = looked_up(starts[..., index])
        at, first = index * size, 0
        for source, last in zip(sources, bounds):

            @pl.when((start >= first) & (start < last))
            def _(source=source, first=first, start=start, at=at):
                rows = source[...] if source.shape[0] == size else source[pl.ds(pl.multiple_of(start - first, size), size)]
                stack[at : at + size], stack[depth + at : depth + at + size] = halves(rows)

            first = last


def product_kernel(starts, size, bounds, parts, split, *refs):
    count = len(bounds)
    sources, refs = refs[:count], refs[count:]
    columns, refs = refs[: 1 if split else 2 * parts], refs[1 if split else 2 * parts :]
    if starts is None:
        (stack,) = sources
    else:
        *refs, stack, raw, sems = refs
        if split:
            split_rows(starts, size, bounds, sources, stack)
        else:
            fetch_rows(starts, size, bounds, sources, stack, raw, sems)
    outs = refs[-parts - (2 if split else 0) :]
    for part in range(parts):
        width = outs[part].shape[1]
        tile = min(LANES, width)
        for at in range(0, width, tile):
            here = slice(at, at + tile)
            if split:
                first = pl.multiple_of(side(split - 1) * width + at, tile)
                high, low = halves(columns[0][:, pl.ds(first, tile)])
                outs[1][:, here], outs[2][:, here] = high, low
            else:
                high, low = (ref[:, here] for ref in columns[2 * part : 2 * part + 2])
            outs[part][:, here] = times(stack, high, low)


def product(sources, starts, size, columns, split, keep, *after):
    again = starts is None
    depth = sources[0].shape[0] // 2 if again else starts.shape[-1] * size
    inner, width = columns[0].shape
    parts = max(len(columns) // 2, 1)
    width = width // 2 if split else width
    anywhere, whole = pl.BlockSpec(memory_space=pl.ANY), pl.BlockSpec(memory_space=pltpu.VMEM)
    outs = [jax.ShapeDtypeStruct((depth, width), jnp.float32)] * parts
    outs += [jax.ShapeDtypeStruct((inner, width), jnp.bfloat16)] * (2 if split else 0)
    scratch = []
    if not again:
        scratch = [pltpu.VMEM((depth, inner), jnp.float32), pltpu.SemaphoreType.DMA((starts.shape[-1],))]
        if keep:
            outs += [jax.ShapeDtypeStruct((2 * depth, inner), jnp.bfloat16)]
        else:
            scratch.insert(0, pltpu.VMEM((2 * depth, inner), jnp.bfloat16))
    bounds = list(np.cumsum([s.shape[0] for s in sources]))
    return pl.pallas_call(
        functools.partial(product_kernel, starts, size, bounds, parts, split),
        out_shape=outs,
        in_specs=[whole if again or split else anywhere] * len(sources) + [whole] * len(columns) + [anywhere] * len(after),
        out_specs=[whole] * len(outs),
        scratch_shapes=scratch,
        compiler_params=pltpu.CompilerParams(vmem_limit_bytes=16 * MIB),
        cost_estimate=pl.CostEstimate(
            flops=6 * depth * inner * width * parts,
            bytes_accessed=4 * depth * inner + 4 * (inner + depth) * width * parts,
            transcendentals=0,
        ),
        name="product",
    )(*sources, *columns, *after)


def finish_kernel(*refs):
    out_ref = refs[-1]
    for part in range(2):
        above, below, own = refs[3 * part : 3 * part + 3]
        width = own.shape[1]
        columns = pl.ds(pl.multiple_of(side(part) * width, width), width)
        out_ref[:, columns] = (above[...] + below[...]) + own[...]


def finish(*values):
    depth, width = values[0].shape
    return pl.pallas_call(
        finish_kernel,
        out_shape=jax.ShapeDtypeStruct((depth, 2 * width), jnp.float32),
        in_specs=[pl.BlockSpec(memory_space=pltpu.VMEM)] * 6,
        out_specs=pl.BlockSpec(memory_space=pltpu.VMEM),
        compiler_params=pltpu.CompilerParams(vmem_limit_bytes=8 * MIB),
        name="finish",
    )(*values)


def plan(order, rows, cols, size, chunks):
    place = np.zeros(rows, np.int64)
    place[order] = np.arange(rows)
    each, half = rows // cols, rows // 2
    needs = np.zeros((rows, cols, rows), np.int64)
    for core in range(cols):
        ways = (-1, 1) if core == 0 else (1, -1)
        steps = [half] + [way * (half - step) for step in range(1, half) for way in ways] + [0]
        for row in range(rows):
            needs[row, core] = [order[(place[row] + step) % rows] for step in steps]
    spots = [(2 * sum(chunks[:chunk]) + at, count) for chunk, count in enumerate(chunks) for at in range(count)]
    taken = np.zeros((rows, cols, rows), np.int64)
    given = np.zeros((rows, cols, each), np.int64)
    for row in range(rows):
        for core in range(cols):
            sent = [block for block in needs[row, cols - 1 - core] if block // each == core]
            given[row, core] = [(block - core * each) * size for block in sent]
            arrived = 0
            for k, block in enumerate(needs[row, core]):
                if block // each == core:
                    taken[row, core, k] = spots[sent.index(block)][0] * size
                else:
                    taken[row, core, k] = sum(spots[arrived]) * size
                    arrived += 1
    return taken, given


def solution(mesh):
    rows, cols = mesh.shape["row"], mesh.shape["col"]
    order = ring_order(mesh)
    group = max(rows // CALLS, 1)
    half = rows // 2
    swap = [(core, cols - 1 - core) for core in range(cols)]
    ways = [
        [
            (order[i] * cols + core, order[(i + (way if core else -way)) % rows] * cols + core)
            for i in range(rows)
            for core in range(cols)
        ]
        for way in (1, -1)
    ]

    def shards(inductance, current_rates):
        size = inductance.shape[0] * cols // rows
        spare = int(group > 1)
        chunks = [group + spare] + [group] * (rows // cols // group - 2) + [group - spare]
        taken, given = plan(order, rows, cols, size, chunks)
        sources, pairs, calls, stacks, made = [], {}, {}, {}, []

        def fetch(first, last, room, *after):
            wanted = slice(sum(chunks[:first]), sum(chunks[:last]))
            for own in pick(inductance, given[..., wanted], size, chunks[first:last], room, *after):
                sources.extend([own, lax.ppermute(own, "col", swap)])

        def term(index, part):
            call, at = divmod(index, group)
            if (call, part) not in calls:
                parts = [part] if call < 3 else [0, 1]
                starts = taken[..., call * group : (call + 1) * group]
                firsts = np.cumsum([0] + [each.shape[0] for each in sources])
                have = sources[: int(np.searchsorted(firsts, starts.max(), "right"))]
                if call in stacks:
                    have, starts = [stacks[call]], None
                keep = call < 3 and call not in stacks
                split = 0 if part in pairs else 1 + part
                columns = [current_rates] if split else [half for each in parts for half in pairs[each]]
                got = product(have, starts, size, columns, split, keep, *made[-1:])
                if split:
                    pairs[part] = got[1:3]
                if keep:
                    stacks[call] = got[-1]
                calls.update({(call, each): value for each, value in zip(parts, got)})
                made.append(got[0])
            return calls[call, part][at * size : (at + 1) * size]

        fetch(0, 1, 52)
        fetch(1, len(chunks), 48, sources[0])

        sums = [[None, None], [None, None]]
        for step in range(half):
            for late in (1, 0):
                for way in range(2):
                    part = (way + late) % 2
                    if step == 0 and late:
                        continue
                    value = term(2 * step - 1 + way if step else 0, part)
                    if sums[way][part] is not None:
                        value = sums[way][part] + value
                    sums[way][part] = lax.ppermute(value, ("row", "col"), ways[way])
        return finish(*(each for part in range(2) for each in (sums[0][part], sums[1][part], term(rows - 1, part))))

    placed = (P(("groups", "col"), "row"), P("row", ("groups", "col")))
    return jax.shard_map(
        shards, mesh=mesh, in_specs=placed, out_specs=P("row", ("groups", "col")), check_vma=False
    )
```

```python
import functools

import jax
import jax.numpy as jnp
import numpy as np
from jax import lax
from jax.experimental import pallas as pl
from jax.experimental.pallas import tpu as pltpu
from jax.sharding import PartitionSpec as P

CALLS = 8
LANES = 512
PIECE = 128
MIB = 2**20


def ring_order(mesh):
    count = mesh.shape["row"]
    axes = list(mesh.axis_names)
    line = np.moveaxis(mesh.devices, axes.index("row"), 0).reshape(count, -1)[:, 0]
    spots = [tuple(device.coords) for device in line]
    moving = [axis for axis in range(3) if len({spot[axis] for spot in spots}) > 1]
    plain = list(range(count))
    if len(moving) != 2:
        return plain
    for outer, inner in (moving, moving[::-1]):
        across = sorted({spot[outer] for spot in spots})
        along = sorted({spot[inner] for spot in spots})
        if len(across) % 2 or len(across) * len(along) != count:
            continue
        at = {(spot[outer], spot[inner]): index for index, spot in enumerate(spots)}
        walk = [at[across[0], along[0]]]
        for turn, a in enumerate(across):
            rest = along[1:]
            walk += [at[a, b] for b in (rest if turn % 2 == 0 else rest[::-1])]
        walk += [at[a, along[0]] for a in across[:0:-1]]
        return walk
    return plain


def looked_up(table):
    row, col = lax.axis_index("row"), lax.axis_index("col")
    found = jnp.int32(0)
    for r in range(table.shape[0]):
        for c in range(table.shape[1]):
            found = jnp.where((row == r) & (col == c), jnp.int32(table[r, c]), found)
    return found


def pick_kernel(starts, size, chunks, a_ref, *refs):
    outs, sems = refs[-1 - len(chunks) : -1], refs[-1]
    spots = [(chunk, at * size) for chunk, count in enumerate(chunks) for at in range(count)]
    piece = min(size, PIECE)
    for index, (chunk, first) in enumerate(spots):
        start = looked_up(starts[..., index])
        for at in range(0, size, piece):
            pltpu.make_async_copy(
                a_ref.at[pl.ds(pl.multiple_of(start + at, piece), piece)],
                outs[chunk].at[pl.ds(first + at, piece)],
                sems.at[chunk],
            ).start()
    for chunk, out_ref in enumerate(outs):
        pltpu.make_async_copy(a_ref.at[pl.ds(0, out_ref.shape[0])], out_ref, sems.at[chunk]).wait()


def pick(inductance, starts, size, chunks, room, *after):
    width = inductance.shape[1]
    moved = 8 * sum(chunks) * size * width
    return pl.pallas_call(
        functools.partial(pick_kernel, starts, size, chunks),
        out_shape=[jax.ShapeDtypeStruct((count * size, width), jnp.float32) for count in chunks],
        in_specs=[pl.BlockSpec(memory_space=pl.ANY)] * (1 + len(after)),
        out_specs=[pl.BlockSpec(memory_space=pltpu.VMEM)] * len(chunks),
        scratch_shapes=[pltpu.SemaphoreType.DMA((len(chunks),))],
        compiler_params=pltpu.CompilerParams(vmem_limit_bytes=room * MIB),
        cost_estimate=pl.CostEstimate(flops=0, bytes_accessed=moved, transcendentals=0),
        name="pick",
    )(inductance, *after)


def side(part):
    return jnp.where((lax.axis_index("col") == 0) == (part == 0), 1, 0)


def halves(value):
    high = value.astype(jnp.bfloat16)
    return high, (value - high.astype(jnp.float32)).astype(jnp.bfloat16)


def times(stack, high, low):
    depth = stack.shape[0] // 2
    both = jnp.dot(stack[...], high, preferred_element_type=jnp.float32)
    rest = jnp.dot(stack[:depth], low, preferred_element_type=jnp.float32)
    return both[:depth] + (both[depth:] + rest)


def fetch_rows(starts, size, bounds, sources, stack, raw, sems):
    for index in range(starts.shape[-1]):
        start = looked_up(starts[..., index])
        first = 0
        for source, last in zip(sources, bounds):

            @pl.when((start >= first) & (start < last))
            def _(source=source, first=first, start=start, index=index):
                pltpu.make_async_copy(
                    source.at[pl.ds(pl.multiple_of(start - first, size), size)],
                    raw.at[pl.ds(index * size, size)],
                    sems.at[index],
                ).start()

            first = last
    for index in range(starts.shape[-1]):
        pltpu.make_async_copy(
            sources[0].at[pl.ds(0, size)], raw.at[pl.ds(index * size, size)], sems.at[index]
        ).wait()
    depth = raw.shape[0]
    stack[:depth], stack[depth:] = halves(raw[...])


def split_rows(starts, size, bounds, sources, stack):
    depth = stack.shape[0] // 2
    for index in range(starts.shape[-1]):
        start = looked_up(starts[..., index])
        at, first = index * size, 0
        for source, last in zip(sources, bounds):

            @pl.when((start >= first) & (start < last))
            def _(source=source, first=first, start=start, at=at):
                rows = source[...] if source.shape[0] == size else source[pl.ds(pl.multiple_of(start - first, size), size)]
                stack[at : at + size], stack[depth + at : depth + at + size] = halves(rows)

            first = last


def product_kernel(starts, size, bounds, parts, split, *refs):
    count = len(bounds)
    sources, refs = refs[:count], refs[count:]
    columns, refs = refs[: 1 if split else 2 * parts], refs[1 if split else 2 * parts :]
    if starts is None:
        (stack,) = sources
    else:
        *refs, stack, raw, sems = refs
        if split:
            split_rows(starts, size, bounds, sources, stack)
        else:
            fetch_rows(starts, size, bounds, sources, stack, raw, sems)
    outs = refs[-parts - (2 if split else 0) :]
    for part in range(parts):
        width = outs[part].shape[1]
        tile = min(LANES, width)
        for at in range(0, width, tile):
            here = slice(at, at + tile)
            if split:
                first = pl.multiple_of(side(split - 1) * width + at, tile)
                high, low = halves(columns[0][:, pl.ds(first, tile)])
                outs[1][:, here], outs[2][:, here] = high, low
            else:
                high, low = (ref[:, here] for ref in columns[2 * part : 2 * part + 2])
            outs[part][:, here] = times(stack, high, low)


def product(sources, starts, size, columns, split, keep, *after):
    again = starts is None
    depth = sources[0].shape[0] // 2 if again else starts.shape[-1] * size
    inner, width = columns[0].shape
    parts = max(len(columns) // 2, 1)
    width = width // 2 if split else width
    anywhere, whole = pl.BlockSpec(memory_space=pl.ANY), pl.BlockSpec(memory_space=pltpu.VMEM)
    outs = [jax.ShapeDtypeStruct((depth, width), jnp.float32)] * parts
    outs += [jax.ShapeDtypeStruct((inner, width), jnp.bfloat16)] * (2 if split else 0)
    scratch = []
    if not again:
        scratch = [pltpu.VMEM((depth, inner), jnp.float32), pltpu.SemaphoreType.DMA((starts.shape[-1],))]
        if keep:
            outs += [jax.ShapeDtypeStruct((2 * depth, inner), jnp.bfloat16)]
        else:
            scratch.insert(0, pltpu.VMEM((2 * depth, inner), jnp.bfloat16))
    bounds = list(np.cumsum([s.shape[0] for s in sources]))
    return pl.pallas_call(
        functools.partial(product_kernel, starts, size, bounds, parts, split),
        out_shape=outs,
        in_specs=[whole if again or split else anywhere] * len(sources) + [whole] * len(columns) + [anywhere] * len(after),
        out_specs=[whole] * len(outs),
        scratch_shapes=scratch,
        compiler_params=pltpu.CompilerParams(vmem_limit_bytes=16 * MIB),
        cost_estimate=pl.CostEstimate(
            flops=6 * depth * inner * width * parts,
            bytes_accessed=4 * depth * inner + 4 * (inner + depth) * width * parts,
            transcendentals=0,
        ),
        name="product",
    )(*sources, *columns, *after)


def finish_kernel(*refs):
    out_ref = refs[-1]
    for part in range(2):
        above, below, own = refs[3 * part : 3 * part + 3]
        width = own.shape[1]
        columns = pl.ds(pl.multiple_of(side(part) * width, width), width)
        out_ref[:, columns] = (above[...] + below[...]) + own[...]


def finish(*values):
    depth, width = values[0].shape
    return pl.pallas_call(
        finish_kernel,
        out_shape=jax.ShapeDtypeStruct((depth, 2 * width), jnp.float32),
        in_specs=[pl.BlockSpec(memory_space=pltpu.VMEM)] * 6,
        out_specs=pl.BlockSpec(memory_space=pltpu.VMEM),
        compiler_params=pltpu.CompilerParams(vmem_limit_bytes=8 * MIB),
        name="finish",
    )(*values)


def plan(order, rows, cols, size, chunks):
    place = np.zeros(rows, np.int64)
    place[order] = np.arange(rows)
    each, half = rows // cols, rows // 2
    needs = np.zeros((rows, cols, rows), np.int64)
    for core in range(cols):
        ways = (-1, 1) if core == 0 else (1, -1)
        steps = [half] + [way * (half - step) for step in range(1, half) for way in ways] + [0]
        for row in range(rows):
            needs[row, core] = [order[(place[row] + step) % rows] for step in steps]
    spots = [(2 * sum(chunks[:chunk]) + at, count) for chunk, count in enumerate(chunks) for at in range(count)]
    taken = np.zeros((rows, cols, rows), np.int64)
    given = np.zeros((rows, cols, each), np.int64)
    for row in range(rows):
        for core in range(cols):
            sent = [block for block in needs[row, cols - 1 - core] if block // each == core]
            given[row, core] = [(block - core * each) * size for block in sent]
            arrived = 0
            for k, block in enumerate(needs[row, core]):
                if block // each == core:
                    taken[row, core, k] = spots[sent.index(block)][0] * size
                else:
                    taken[row, core, k] = sum(spots[arrived]) * size
                    arrived += 1
    return taken, given


def solution(mesh):
    rows, cols = mesh.shape["row"], mesh.shape["col"]
    order = ring_order(mesh)
    group = max(rows // CALLS, 1)
    half = rows // 2
    swap = [(core, cols - 1 - core) for core in range(cols)]
    ways = [
        [
            (order[i] * cols + core, order[(i + (way if core else -way)) % rows] * cols + core)
            for i in range(rows)
            for core in range(cols)
        ]
        for way in (1, -1)
    ]

    def shards(inductance, current_rates):
        size = inductance.shape[0] * cols // rows
        spare = int(group > 1)
        chunks = [group + spare] + [group] * (rows // cols // group - 2) + [group - spare]
        taken, given = plan(order, rows, cols, size, chunks)
        sources, pairs, calls, stacks, made = [], {}, {}, {}, []

        def fetch(first, last, room, *after):
            wanted = slice(sum(chunks[:first]), sum(chunks[:last]))
            for own in pick(inductance, given[..., wanted], size, chunks[first:last], room, *after):
                sources.extend([own, lax.ppermute(own, "col", swap)])

        def term(index, part):
            call, at = divmod(index, group)
            if (call, part) not in calls:
                parts = [part] if call < 3 else [0, 1]
                starts = taken[..., call * group : (call + 1) * group]
                firsts = np.cumsum([0] + [each.shape[0] for each in sources])
                have = sources[: int(np.searchsorted(firsts, starts.max(), "right"))]
                if call in stacks:
                    have, starts = [stacks[call]], None
                keep = call < 3 and call not in stacks
                split = 0 if part in pairs else 1 + part
                columns = [current_rates] if split else [half for each in parts for half in pairs[each]]
                got = product(have, starts, size, columns, split, keep, *made[-1:])
                if split:
                    pairs[part] = got[1:3]
                if keep:
                    stacks[call] = got[-1]
                calls.update({(call, each): value for each, value in zip(parts, got)})
                made.append(got[0])
            return calls[call, part][at * size : (at + 1) * size]

        fetch(0, 1, 52)
        fetch(1, len(chunks), 48, sources[0])

        sums = [[None, None], [None, None]]
        for step in range(half):
            for late in (1, 0):
                for way in range(2):
                    part = (way + late) % 2
                    if step == 0 and late:
                        continue
                    value = term(2 * step - 1 + way if step else 0, part)
                    if sums[way][part] is not None:
                        value = sums[way][part] + value
                    sums[way][part] = lax.ppermute(value, ("row", "col"), ways[way])
        return finish(*(each for part in range(2) for each in (sums[0][part], sums[1][part], term(rows - 1, part))))

    placed = (P(("groups", "col"), "row"), P("row", ("groups", "col")))
    return jax.shard_map(
        shards, mesh=mesh, in_specs=placed, out_specs=P("row", ("groups", "col")), check_vma=False
    )
```
